32 devices in a mesh: pw: 2 (over x), band: 16 (over z, y, core).
Axes of the slice: x: 2, y: 2, z: 4, core: 2. Of those that a mesh axis runs over, the one named last changes fastest.
Arguments:
- stick_coefs: float32 [16, 2, 48, 256], P('band', None, None, 'pw'), may hold values from -6 to 6
- miller: int32 [2, 256], P(None, 'pw'), may hold values from 0 to 47, as said below
- stick_count: int32 [2], P('pw'), may hold values from 1 to 128, as said below
Outputs:
- exchange_coefs: float32 [16, 2, 48, 256], P('band', None, None, 'pw')
The draws below stay inside these ranges and needn't reach their ends.
Inputs may be any that keep to these rules, and one draw needn't show every extreme that they name: `stick_count`: some pw index has exactly 128 live sticks. Over the live slots the columns (miller[0, s], miller[1, s]) are distinct and are the columns of smallest sigma(miller[0])**2 + sigma(miller[1])**2, as many as there are live slots (ties at the edge broken arbitrarily); the other slots hold arbitrary columns.
All inputs are finite; a program needn't handle non-finite values.
Results may differ from the reference program's by a relative error of at most 0.0003.
Values sent between devices are 32-bit elements; how exact they have to be, the bound alone decides.
No kernel may reach another device: no remote copies, remote signals or barrier semaphores. Data moves between devices by JAX's collectives and lax.ppermute only.
A program may use at most 64 MiB of HBM per device.

```python
import math
import jax
import jax.numpy as jnp
from jax import lax

NGRID = 48
STK_DEV = 128
ORB_DEV = 1
HALF = 2
NG = 16
NMEM = 2
STICKS = 256


def stick_plan(key):
    subkeys = jax.random.split(jax.random.fold_in(key, 5183), 5)
    owners = STICKS // STK_DEV
    counts = jax.random.randint(subkeys[0], (owners,), STK_DEV // 8, STK_DEV + 1)
    fullest = jax.random.randint(subkeys[1], (), 0, owners)
    counts = jnp.where(jnp.arange(owners) == fullest, STK_DEV, counts).astype(jnp.int32)
    live_total = jnp.sum(counts)
    columns = NGRID * NGRID
    col_ids = jnp.arange(columns, dtype=jnp.int32)
    first_index = col_ids // NGRID
    second_index = col_ids % NGRID
    signed_first = jnp.where(first_index < NGRID // 2, first_index, first_index - NGRID)
    signed_second = jnp.where(second_index < NGRID // 2, second_index, second_index - NGRID)
    radius = signed_first * signed_first + signed_second * signed_second
    tiebreak = jax.random.permutation(subkeys[2], columns).astype(jnp.int32)
    by_radius = jnp.argsort(radius * columns + tiebreak, stable=True)
    shuffle = jax.random.permutation(subkeys[3], columns).astype(jnp.int32)
    position = jnp.arange(columns, dtype=jnp.int32)
    shuffle_score = jnp.where(position < live_total, shuffle, columns + position)
    picked = by_radius[jnp.argsort(shuffle_score, stable=True)]
    slot_ids = jnp.arange(STICKS, dtype=jnp.int32)
    slot_owner = slot_ids // STK_DEV
    slot_pos = slot_ids % STK_DEV
    offsets = jnp.cumsum(counts) - counts
    live_rank = jnp.minimum(offsets[slot_owner] + slot_pos, columns - 1)
    live_slot = slot_pos < counts[slot_owner]
    filler = jax.random.randint(subkeys[4], (STICKS,), 0, columns)
    column = jnp.where(live_slot, picked[live_rank], filler).astype(jnp.int32)
    miller = jnp.stack([column // NGRID, column % NGRID]).astype(jnp.int32)
    return (counts, miller)


def draw_miller(key, part):
    return stick_plan(key)[1]


def draw_stick_count(key, part):
    return stick_plan(key)[0]


def shard_levels(key, shape, pieces, least, top_value):
    level, own = 1.0, jax.random.fold_in(key, 6)
    for axis_at, parts in pieces:
        steps = jnp.exp(jax.random.uniform(jax.random.fold_in(own, axis_at), (parts,), jnp.float32, least / len(pieces), top_value / len(pieces)))
        level = level * jnp.repeat(steps, shape[axis_at] // parts).reshape([-1 if axis == axis_at else 1 for axis in range(len(shape))])
    return level


def normal_values(own_key, extent, scale, most, pieces=(), kind=jnp.bfloat16):
    drawn = jax.random.normal(own_key, extent, jnp.float32) * scale
    if len(pieces) > 0:
        drawn = shard_levels(own_key, extent, pieces, -0.22, 0.18) * drawn
    return jnp.clip(drawn, min=-most, max=most).astype(kind)


def setup_inputs(seed: int = 0) -> dict:
    arg_keys = jax.random.split(jax.random.key(seed), 4)
    return {
        "stick_coefs": normal_values(arg_keys[0], (NG, NMEM, NGRID, STICKS), 1.0, 6.0, ((0, 16), (3, 2)), jnp.float32),
        "miller": draw_miller(jax.random.fold_in(arg_keys[3], 71), 0),
        "stick_count": draw_stick_count(jax.random.fold_in(arg_keys[3], 71), 0),
    }


kernel_scale = 4.0
screen_width = 16.0

def hartley_axis(cube_field, axis_id):
    spectrum = jnp.fft.fft(cube_field, axis=axis_id)
    return jnp.real(spectrum) - jnp.imag(spectrum)

def hartley_cube(cube_field):
    for axis_id in (-3, -2, -1):
        cube_field = hartley_axis(cube_field, axis_id)
    return cube_field

def coulomb_kernel(points):
    indices = jnp.arange(points)
    signed = jnp.where(indices < points // 2, indices, indices - points).astype(jnp.float32)
    squares = signed * signed
    radius_sq = squares[:, None, None] + squares[None, :, None] + squares[None, None, :]
    scaled = radius_sq / screen_width
    divisor = jnp.where(radius_sq > 0, scaled, jnp.float32(1.0))
    return kernel_scale * jnp.where(radius_sq > 0, -jnp.expm1(-divisor) / divisor, jnp.float32(1.0))

def synthesize(group_coefs, miller, live_mask):
    points = group_coefs.shape[1]
    cube_grid = jnp.zeros((group_coefs.shape[0], points, points, points), jnp.float32)
    cube_grid = cube_grid.at[:, :, miller[0], miller[1]].add(group_coefs * live_mask)
    return hartley_cube(cube_grid) / math.sqrt(points ** 3)

def poisson(density, kernel):
    points = density.shape[-1]
    return hartley_cube(kernel * hartley_cube(density)) / float(points ** 3)

def reference(stick_coefs, miller, stick_count):
    groups = stick_coefs.shape[0]
    members = stick_coefs.shape[1]
    points = stick_coefs.shape[2]
    owners = stick_count.shape[0]
    per_owner = stick_coefs.shape[3] // owners
    position = jnp.arange(per_owner, dtype=jnp.int32)
    live_mask = (position[None, :] < stick_count[:, None]).reshape(-1).astype(jnp.float32)
    kernel = coulomb_kernel(points)

    def group_result(group):
        own_orbs = synthesize(stick_coefs[group], miller, live_mask)
        own_orbs = own_orbs.reshape(owners, ORB_DEV, points, points, points)
        exch_field = jnp.zeros_like(own_orbs)
        for offset in range(-HALF, HALF + 1):
            if offset == 0:
                visitor = own_orbs
            else:
                other = jnp.mod(group + offset, groups).astype(jnp.int32)
                visitor = synthesize(stick_coefs[other], miller, live_mask)
                visitor = visitor.reshape(owners, ORB_DEV, points, points, points)
            for left_idx in range(ORB_DEV):
                for right_idx in range(ORB_DEV):
                    potential = poisson(own_orbs[:, left_idx] * visitor[:, right_idx], kernel)
                    exch_field = exch_field.at[:, left_idx].add(-potential * visitor[:, right_idx])
        exch_field = exch_field.reshape(members, points, points, points)
        spectrum = hartley_cube(exch_field) / math.sqrt(points ** 3)
        return spectrum[:, :, miller[0], miller[1]] * live_mask
    return lax.map(group_result, jnp.arange(groups, dtype=jnp.int32))
```

```python
import functools
import math

import jax
import jax.numpy as jnp
import ml_dtypes
import numpy as np
from jax import lax
from jax.experimental import pallas as pl
from jax.experimental.pallas import tpu as pltpu
from jax.sharding import PartitionSpec as P

HALF = 2
kernel_scale = 4.0
screen_width = 16.0
LANES = 128
ROWS = 16


def round_up(value, unit):
    return -(-value // unit) * unit


def split_table(table):
    head = table.astype(np.float32).astype(ml_dtypes.bfloat16)
    rest = (table - head.astype(np.float64)).astype(np.float32).astype(ml_dtypes.bfloat16)
    return head, rest


@functools.lru_cache(maxsize=None)
def build_tables(points, sticks, members):
    signed = np.arange(points)
    signed = np.where(signed < points // 2, signed, signed - points)
    radius = signed[:, None] ** 2 + signed[None, :] ** 2
    limit = np.sort(radius.reshape(-1))[min(sticks, points * points) - 1]
    picked = sorted({(abs(b), abs(c)) for b in signed for c in signed if b * b + c * c <= limit})
    largest = max(b for b, _ in picked)
    grid = 4 * largest + 1 if 4 * largest + 1 < points else points

    def fold(value):
        value = value % points
        return min(value, points - value)

    pairs = set()
    for b1, c1 in picked:
        for b2, c2 in picked:
            for b in {fold(b1 + b2), fold(b1 - b2)}:
                for c in {fold(c1 + c2), fold(c1 - c2)}:
                    pairs.add((b, c))
    pairs = sorted(pairs)
    near = grid // 2 + 1
    place = [(y, z) for y in range(near) for z in range(near)]
    once = np.array([0.5 if 2 * y % grid == 0 else 1.0 for y in range(near)])
    place_weight = np.array([once[y] * once[z] for y, z in place])

    def wave(kind, freq, spot):
        angle = 2.0 * np.pi * ((freq[:, None] * spot[None, :]) % grid) / grid
        return np.cos(angle) if kind == "c" else np.sin(angle)

    spots = np.array(place)

    def class_waves(freqs):
        freqs = np.array(freqs)
        return [
            wave(ky, freqs[:, 0], spots[:, 0]) * wave(kz, freqs[:, 1], spots[:, 1])
            for ky, kz in ("cc", "sc", "cs", "ss")
        ]

    n_place = round_up(len(place), ROWS)
    n_pairs = round_up(len(pairs), ROWS)
    n_picked = round_up(len(picked), ROWS)

    def stack(tables, rows, cols):
        head = np.zeros((4, rows, 3 * cols), ml_dtypes.bfloat16)
        for at, table in enumerate(tables):
            full = np.zeros((rows, cols))
            full[: table.shape[0], : table.shape[1]] = table
            high, low = split_table(full)
            head[at] = np.concatenate([high, high, low], axis=1)
        return head

    scale = points**-1.5
    small = class_waves(picked)
    large = class_waves(pairs)
    synth = stack([t.T * scale for t in small], n_place, n_picked)
    project = stack(
        [-t * place_weight * scale * (points / grid) ** 2 for t in small], n_picked, n_place
    )
    forward = stack([t * place_weight for t in large], n_pairs, n_place)
    inverse = stack([t.T for t in large], n_place, n_pairs)

    index = np.arange(points)
    angle = 2.0 * np.pi * ((index[:, None] * index[None, :]) % points) / points
    cas = np.cos(angle) + np.sin(angle)
    lanes = round_up(members * points, LANES)
    block = np.zeros((lanes, lanes))
    for member in range(members):
        at = member * points
        block[at : at + points, at : at + points] = cas
    high, low = split_table(block)
    turn_left = np.concatenate([high, high, low], axis=1)
    turn_right = np.block([[high, low], [high, low]])

    squares = signed.astype(np.float64) ** 2
    freqs = np.array(pairs)
    total = (freqs[:, 0] ** 2 + freqs[:, 1] ** 2)[:, None] + squares[None, :]
    scaled = total / screen_width
    safe = np.where(total > 0, scaled, 1.0)
    kernel = kernel_scale * np.where(total > 0, -np.expm1(-safe) / safe, 1.0)
    double = np.where(2 * freqs % grid == 0, 1.0, 2.0)
    kernel = kernel * (double[:, 0] * double[:, 1])[:, None]
    kernel = kernel * (points / grid) ** 2 / float(points**3)
    weights = np.zeros((n_pairs, lanes), np.float32)
    for member in range(members):
        weights[: len(pairs), member * points : (member + 1) * points] = kernel

    codes = np.full((n_picked, LANES), -7.0, np.float32)
    for at, (b, c) in enumerate(picked):
        codes[at] = b * points + c
    return dict(
        synth=synth,
        project=project,
        forward=forward,
        inverse=inverse,
        turn_left=turn_left,
        turn_right=turn_right,
        weights=weights,
        codes=codes,
    )


TABLE_NAMES = (
    "synth",
    "project",
    "forward",
    "inverse",
    "turn_left",
    "turn_right",
    "weights",
    "codes",
)


def dot(left, right):
    return jnp.dot(left, right, preferred_element_type=jnp.float32)


def split(value):
    high = value.astype(jnp.bfloat16)
    low = (value - high.astype(jnp.float32)).astype(jnp.bfloat16)
    return high, low


def stacked(value):
    high, low = split(value)
    return jnp.concatenate([high, low, high], axis=0)


def pick_matrix(indices, codes, points):
    first, second = indices[0:1], indices[1:2]
    alive = first >= 0.0
    signed_first = jnp.where(first < points // 2, first, first - points)
    signed_second = jnp.where(second < points // 2, second, second - points)
    code = jnp.abs(signed_first) * points + jnp.abs(signed_second)
    code = jnp.where(alive, code, -1.0)
    one = jnp.where(codes[:, 0:1] == code, 1.0, 0.0)
    sign_first = jnp.where(signed_first < 0.0, -1.0, 1.0)
    sign_second = jnp.where(signed_second < 0.0, -1.0, 1.0)
    parts = [one, one * sign_first, one * sign_second, one * (sign_first * sign_second)]
    return jnp.concatenate(parts, axis=0).astype(jnp.bfloat16)


def unfold(parts):
    even, odd = parts[0] + parts[2], parts[1] + parts[3]
    even_less, odd_less = parts[0] - parts[2], parts[1] - parts[3]
    return [even + odd, even - odd, even_less + odd_less, even_less - odd_less]


def turn(value, turn_right):
    lanes = turn_right.shape[0] // 2
    outs = []
    for at in range(0, value.shape[1], lanes):
        high, low = split(value[:, at : at + lanes])
        out = dot(jnp.concatenate([high, low], axis=1), turn_right)
        outs.append(out[:, :lanes] + out[:, lanes:])
    return outs[0] if len(outs) == 1 else jnp.concatenate(outs, axis=1)


def each_part(small, body):
    if small:
        for at in range(4):
            body(at)
    else:
        pl.loop(0, 4)(body)


def synthesize(small, blocks, pick, turn_left, synth_ref, coefs_ref, orbs_ref):
    fields = [dot(turn_left, stacked(block)) for block in blocks]
    field = fields[0] if len(fields) == 1 else jnp.concatenate(fields, axis=0)
    high, low = split(field)
    contract = (((1,), (1,)), ((), ()))
    coefs = lax.dot_general(pick, high, contract, preferred_element_type=jnp.float32)
    coefs = coefs + lax.dot_general(pick, low, contract, preferred_element_type=jnp.float32)
    rows = pick.shape[0] // 4
    for at in range(4):
        coefs_ref[at] = coefs[at * rows : (at + 1) * rows]

    def body(at):
        orbs_ref[at] = dot(synth_ref[at], stacked(coefs_ref[at]))

    each_part(small, body)
    for at, quadrant in enumerate(unfold([orbs_ref[at] for at in range(4)])):
        orbs_ref[at] = quadrant


def exchange_kernel(
    members,
    points,
    group_blocks,
    indices_ref,
    *refs,
):
    count = sum(group_blocks)
    coef_refs = refs[:count]
    tables = refs[count : count + len(TABLE_NAMES)]
    synth_ref, project_ref, forward_ref, inverse_ref = tables[:4]
    turn_left_ref, turn_right_ref, weights_ref, codes_ref = tables[4:]
    out_ref, own_ref, visit_ref, field_ref, work_ref, coefs_ref = refs[count + len(TABLE_NAMES) :]
    pick = pick_matrix(indices_ref[...], codes_ref[...], points)
    turn_left, turn_right = turn_left_ref[...], turn_right_ref[...]
    lanes = turn_right.shape[0] // 2
    pad = lanes - members * points
    small = forward_ref.shape[1] <= 512

    def coefs_of(ref):
        block = jnp.concatenate([ref[at] for at in range(ref.shape[0])], axis=1)
        if pad:
            block = jnp.concatenate([block, jnp.zeros((pad, block.shape[1]), block.dtype)], axis=0)
        return block

    synthesize(
        small,
        [coefs_of(coef_refs[0])],
        pick,
        turn_left,
        synth_ref,
        coefs_ref.at[:, :, :lanes],
        own_ref,
    )
    field_ref[...] = jnp.zeros_like(field_ref)
    start = 0
    for size in group_blocks:
        blocks = [coefs_of(ref) for ref in coef_refs[start : start + size]]
        start += size
        wide = size * lanes
        visit, work = visit_ref.at[:, :, :wide], work_ref.at[:, :, :wide]
        synthesize(small, blocks, pick, turn_left, synth_ref, coefs_ref.at[:, :, :wide], visit)

        density = []
        for at in range(4):
            own = own_ref[at]
            both = own if size == 1 else jnp.concatenate([own] * size, axis=1)
            density.append(both * visit[at])
        for at, part in enumerate(unfold(density)):
            work[at] = part

        def poisson(at):
            spectrum = dot(forward_ref[at], stacked(work[at]))
            spectrum = turn(spectrum, turn_right)
            weights = weights_ref[...]
            weights = weights if size == 1 else jnp.concatenate([weights] * size, axis=1)
            spectrum = turn(spectrum * weights, turn_right)
            work[at] = dot(inverse_ref[at], stacked(spectrum))

        each_part(small, poisson)
        for at, quadrant in enumerate(unfold([work[at] for at in range(4)])):
            term = quadrant * visit[at]
            total = term[:, :lanes]
            for block in range(1, size):
                total = total + term[:, block * lanes : (block + 1) * lanes]
            field_ref[at] += total

    field = unfold([field_ref[at] for at in range(4)])
    coefs = [dot(project_ref[at], stacked(field[at])) for at in range(4)]
    coefs = turn(jnp.concatenate(coefs, axis=0), turn_right)
    high, low = split(coefs.T)
    own_pick = pick[:, : out_ref.shape[1]]
    result = dot(high, own_pick) + dot(low, own_pick)
    out_ref[...] = result[: members * points]


def swap(value, axis, partner):
    count = lax.axis_size(axis)
    return lax.ppermute(value, axis, [(at, partner(at) % count) for at in range(count)])


def rest_of_ring(value, axis):
    count = lax.axis_size(axis)
    return [
        lax.ppermute(value, axis, [(at, (at + step) % count) for at in range(count)])
        for step in range(1, count)
    ]


def shards(stick_coefs, miller, stick_count):
    groups, members, points, per_owner = stick_coefs.shape
    owners = lax.axis_size("pw")
    batch = max(n for n in range(1, members + 1) if members % n == 0 and (n == 1 or n * points <= LANES))
    tables = build_tables(points, per_owner * owners, batch)
    position = jnp.arange(per_owner, dtype=jnp.int32)[None]
    indices = jnp.where(position < stick_count[0], miller, -1).astype(jnp.float32)
    own = stick_coefs.reshape(members * points, per_owner)
    load = jnp.concatenate([own, indices, jnp.zeros((6, per_owner), jnp.float32)], axis=0)
    loads = [load] + rest_of_ring(load, "pw")
    coefs = jnp.stack([part[: members * points] for part in loads])
    indices = jnp.concatenate([part[members * points :] for part in loads], axis=1)

    ring = lax.axis_size("band")
    mate = swap(coefs, "band", lambda at: at ^ 1)
    near = swap(coefs, "band", lambda at: at ^ 2)
    far = swap(coefs, "band", lambda at: at + 2 if at & 2 else at - 2 + ring)
    me = lax.axis_index("band")
    near_goes = (me & 1) == ((me >> 1) & 1)
    last = swap(jnp.where(near_goes, near, far), "band", lambda at: at ^ 1)

    lanes = tables["turn_right"].shape[0] // 2
    n_place, n_picked = tables["synth"].shape[1], tables["project"].shape[1]
    blocks = (2, 2, 1)
    vmem = pl.BlockSpec(memory_space=pltpu.VMEM)
    values = [jnp.asarray(tables[name]) for name in TABLE_NAMES]

    def exchange(pieces):
        return pl.pallas_call(
            functools.partial(exchange_kernel, batch, points, blocks),
            out_shape=jax.ShapeDtypeStruct((batch * points, per_owner), jnp.float32),
            in_specs=[vmem] * (1 + len(pieces) + len(values)),
            out_specs=vmem,
            scratch_shapes=[
                pltpu.VMEM((4, n_place, lanes), jnp.float32),
                pltpu.VMEM((4, n_place, 2 * lanes), jnp.float32),
                pltpu.VMEM((4, n_place, lanes), jnp.float32),
                pltpu.VMEM((4, n_place, 2 * lanes), jnp.float32),
                pltpu.VMEM((4, n_picked, 2 * lanes), jnp.float32),
            ],
            compiler_params=pltpu.CompilerParams(vmem_limit_bytes=50 * 2**20),
        )(indices, *pieces, *values)

    pieces = (coefs, mate, near, far, last)
    if batch == members:
        result = exchange(pieces)
    else:
        cut = lambda piece: piece.reshape(owners, -1, batch * points, per_owner).swapaxes(0, 1)
        result = lax.map(exchange, tuple(cut(piece) for piece in pieces))
    return result.reshape(groups, members, points, per_owner)


def solution(mesh):
    return jax.shard_map(
        shards,
        mesh=mesh,
        in_specs=(P("band", None, None, "pw"), P(None, "pw"), P("pw")),
        out_specs=P("band", None, None, "pw"),
        check_vma=False,
    )
```

```python
import functools
import math

import jax
import jax.numpy as jnp
import ml_dtypes
import numpy as np
from jax import lax
from jax.experimental import pallas as pl
from jax.experimental.pallas import tpu as pltpu
from jax.sharding import PartitionSpec as P

HALF = 2
kernel_scale = 4.0
screen_width = 16.0
LANES = 128
ROWS = 16
SMALL = 512


def round_up(value, unit):
    return -(-value // unit) * unit


def split_table(table):
    head = table.astype(np.float32).astype(ml_dtypes.bfloat16)
    rest = (table - head.astype(np.float64)).astype(np.float32).astype(ml_dtypes.bfloat16)
    return head, rest


@functools.lru_cache(maxsize=None)
def build_tables(points, sticks, members):
    signed = np.arange(points)
    signed = np.where(signed < points // 2, signed, signed - points)
    radius = signed[:, None] ** 2 + signed[None, :] ** 2
    limit = np.sort(radius.reshape(-1))[min(sticks, points * points) - 1]
    picked = sorted({(abs(b), abs(c)) for b in signed for c in signed if b * b + c * c <= limit})
    largest = max(b for b, _ in picked)
    grid = 4 * largest + 1 if 4 * largest + 1 < points else points

    def fold(value):
        value = value % points
        return min(value, points - value)

    pairs = set()
    for b1, c1 in picked:
        for b2, c2 in picked:
            for b in {fold(b1 + b2), fold(b1 - b2)}:
                for c in {fold(c1 + c2), fold(c1 - c2)}:
                    pairs.add((b, c))
    pairs = sorted(pairs)
    near = grid // 2 + 1
    place = [(y, z) for y in range(near) for z in range(near)]
    once = np.array([0.5 if 2 * y % grid == 0 else 1.0 for y in range(near)])
    place_weight = np.array([once[y] * once[z] for y, z in place])

    def wave(kind, freq, spot):
        angle = 2.0 * np.pi * ((freq[:, None] * spot[None, :]) % grid) / grid
        return np.cos(angle) if kind == "c" else np.sin(angle)

    spots = np.array(place)

    def class_waves(freqs):
        freqs = np.array(freqs)
        return [
            wave(ky, freqs[:, 0], spots[:, 0]) * wave(kz, freqs[:, 1], spots[:, 1])
            for ky, kz in ("cc", "sc", "cs", "ss")
        ]

    n_place = round_up(len(place), ROWS)
    n_pairs = round_up(len(pairs), ROWS)
    n_picked = round_up(len(picked), ROWS)

    def stack(tables, rows, cols):
        full = np.zeros((4, rows, cols))
        for at, table in enumerate(tables):
            full[at, : table.shape[0], : table.shape[1]] = table
        high, low = split_table(full)
        return np.concatenate([high, high, low], axis=2)

    scale = points**-1.5
    small = class_waves(picked)
    large = class_waves(pairs)
    synth = stack([t.T * scale for t in small], n_place, n_picked)
    project = stack(
        [-t * place_weight * scale * (points / grid) ** 2 for t in small], n_picked, n_place
    )
    forward = stack([t * place_weight for t in large], n_pairs, n_place)
    inverse = stack([t.T for t in large], n_place, n_pairs)

    index = np.arange(points)
    angle = 2.0 * np.pi * ((index[:, None] * index[None, :]) % points) / points
    cas = np.cos(angle) + np.sin(angle)
    lanes = round_up(members * points, LANES)
    block = np.zeros((lanes, lanes))
    for member in range(members):
        at = member * points
        block[at : at + points, at : at + points] = cas
    high, low = split_table(block)
    turn_left = np.concatenate([high, high, low], axis=1)
    turn_right = np.block([[high, low], [high, low]])

    squares = signed.astype(np.float64) ** 2
    freqs = np.array(pairs)
    total = (freqs[:, 0] ** 2 + freqs[:, 1] ** 2)[:, None] + squares[None, :]
    scaled = total / screen_width
    safe = np.where(total > 0, scaled, 1.0)
    kernel = kernel_scale * np.where(total > 0, -np.expm1(-safe) / safe, 1.0)
    double = np.where(2 * freqs % grid == 0, 1.0, 2.0)
    kernel = kernel * (double[:, 0] * double[:, 1])[:, None]
    kernel = kernel * (points / grid) ** 2 / float(points**3)
    weights = np.zeros((n_pairs, lanes))
    for member in range(members):
        weights[: len(pairs), member * points : (member + 1) * points] = kernel

    codes = np.full((n_picked, LANES), -7.0)
    for at, (b, c) in enumerate(picked):
        codes[at, 0], codes[at, 1] = b, c
    return dict(
        synth=synth,
        project=project,
        forward=forward,
        inverse=inverse,
        turn_left=turn_left,
        turn_right=turn_right,
        weights=np.concatenate(split_table(weights), axis=1),
        codes=codes.astype(ml_dtypes.bfloat16),
    )


def pack_tables(tables):
    shelves = (("forward",), ("project",), ("inverse", "synth"))
    shelves += (("turn_left", "turn_right", "weights", "codes"),)
    flat = {name: table.reshape(-1, table.shape[-1]) for name, table in tables.items()}
    where, row, width = {}, 0, 0
    for shelf in shelves:
        column = 0
        for name in shelf:
            where[name] = (row, column)
            column += round_up(flat[name].shape[1], LANES)
        row += round_up(max(flat[name].shape[0] for name in shelf), ROWS)
        width = max(width, column)
    packed = np.zeros((row, width), ml_dtypes.bfloat16)
    for name, (first, column) in where.items():
        rows, cols = flat[name].shape
        packed[first : first + rows, column : column + cols] = flat[name]
    return packed, where


def table_getter(shapes, refs, where):
    def get(name, at=None):
        shape = shapes[name]
        if where is None:
            ref = refs[TABLE_NAMES.index(name)]
            return ref[...] if at is None else ref[at]
        first, column = where[name]
        rows = shape[-2]
        first = first if at is None else first + at * rows
        return refs[0][first : first + rows, column : column + shape[-1]]

    return get


TABLE_NAMES = (
    "synth",
    "project",
    "forward",
    "inverse",
    "turn_left",
    "turn_right",
    "weights",
    "codes",
)


def dot(left, right):
    return jnp.dot(left, right, preferred_element_type=jnp.float32)


def split(value):
    high = value.astype(jnp.bfloat16)
    low = (value - high.astype(jnp.float32)).astype(jnp.bfloat16)
    return high, low


def stacked(value):
    high, low = split(value)
    return jnp.concatenate([high, low, high], axis=0)


def product(table, value):
    return dot(table, stacked(value))


def pick_matrix(indices, codes, points):
    first, second = indices[0:1], indices[1:2]
    alive = first >= 0.0
    signed_first = jnp.where(first < points // 2, first, first - points)
    signed_second = jnp.where(second < points // 2, second, second - points)
    first_same = codes[:, 0:1] == jnp.where(alive, jnp.abs(signed_first), -1.0)
    one = jnp.where(first_same & (codes[:, 1:2] == jnp.abs(signed_second)), 1.0, 0.0)
    sign_first = jnp.where(signed_first < 0.0, -1.0, 1.0)
    sign_second = jnp.where(signed_second < 0.0, -1.0, 1.0)
    parts = [one, one * sign_first, one * sign_second, one * (sign_first * sign_second)]
    return jnp.concatenate(parts, axis=0).astype(jnp.bfloat16)


def unfold(parts):
    even, odd = parts[0] + parts[2], parts[1] + parts[3]
    even_less, odd_less = parts[0] - parts[2], parts[1] - parts[3]
    return [even + odd, even - odd, even_less + odd_less, even_less - odd_less]


def turn(value, turn_right):
    lanes = turn_right.shape[0] // 2
    outs = []
    for at in range(0, value.shape[1], lanes):
        high, low = split(value[:, at : at + lanes])
        out = dot(jnp.concatenate([high, low], axis=1), turn_right)
        outs.append(out[:, :lanes] + out[:, lanes:])
    return outs[0] if len(outs) == 1 else jnp.concatenate(outs, axis=1)


def each_part(small, body):
    if small:
        for at in range(4):
            body(at)
    else:
        pl.loop(0, 4)(body)


def synthesize(small, blocks, pick, get, coefs_ref, orbs_ref):
    turn_left = get("turn_left")
    fields = [dot(turn_left, stacked(block)) for block in blocks]
    field = fields[0] if len(fields) == 1 else jnp.concatenate(fields, axis=0)
    high, low = split(field)
    contract = (((1,), (1,)), ((), ()))
    coefs = lax.dot_general(pick, high, contract, preferred_element_type=jnp.float32)
    coefs = coefs + lax.dot_general(pick, low, contract, preferred_element_type=jnp.float32)
    rows = pick.shape[0] // 4
    for at in range(4):
        coefs_ref[at] = coefs[at * rows : (at + 1) * rows]

    def body(at):
        orbs_ref[at] = product(get("synth", at), coefs_ref[at])

    each_part(small, body)
    for at, quadrant in enumerate(unfold([orbs_ref[at] for at in range(4)])):
        orbs_ref[at] = quadrant


def exchange_kernel(members, points, sizes, begins, ends, shapes, where, *refs):
    refs = list(refs)
    take = lambda count: [refs.pop(0) for _ in range(count)]
    prior_ref = None
    if begins:
        indices_ref, flag_in_ref = take(2)
    else:
        pick_ref, own_ref, prior_ref = take(3)
    coef_refs = take(sum(sizes))
    get = table_getter(shapes, take(len(TABLE_NAMES) if where is None else 1), where)
    if ends:
        (out_ref,) = take(1)
    elif begins:
        pick_ref, own_ref, field_ref, flag_ref = take(4)
        flag_ref[...] = flag_in_ref[...]
    else:
        (field_ref,) = take(1)
    visit_all_ref, work_all_ref, coefs_all_ref = take(3)
    if begins and ends:
        pick_ref, own_ref, field_ref = take(3)
    if begins:
        pick_ref[...] = pick_matrix(indices_ref[...], get("codes").astype(jnp.float32), points)
    pick, turn_right = pick_ref[...], get("turn_right")
    lanes = turn_right.shape[0] // 2
    pad = lanes - members * points
    small = where is not None

    def coefs_of(ref):
        block = jnp.concatenate([ref[at] for at in range(ref.shape[0])], axis=1)
        if pad:
            block = jnp.concatenate([block, jnp.zeros((pad, block.shape[1]), block.dtype)], axis=0)
        return block

    weight = get("weights").astype(jnp.float32)
    weight = weight[:, :lanes] + weight[:, lanes:]
    start = 0
    for step, size in enumerate(sizes):
        refs = [ref.at[:, :, : size * lanes] for ref in (visit_all_ref, work_all_ref, coefs_all_ref)]
        visit_ref, work_ref, coefs_ref = refs
        blocks = [coefs_of(ref) for ref in coef_refs[start : start + size]]
        start += size
        synthesize(small, blocks, pick, get, coefs_ref, visit_ref)
        if begins and step == 0:
            for at in range(4):
                own_ref[at] = visit_ref[at, :, :lanes]
        weights = jnp.concatenate([weight] * size, axis=1)
        density = []
        for at in range(4):
            density.append(jnp.concatenate([own_ref[at]] * size, axis=1) * visit_ref[at])
        density = unfold(density)
        if small:
            spectra = [product(get("forward", at), density[at]) for at in range(4)]
            spectrum = turn(jnp.concatenate(spectra, axis=0), turn_right)
            spectrum = turn(spectrum * jnp.concatenate([weights] * 4, axis=0), turn_right)
            rows = weights.shape[0]
            potential = [
                product(get("inverse", at), spectrum[at * rows : (at + 1) * rows]) for at in range(4)
            ]
        else:
            for at, part in enumerate(density):
                work_ref[at] = part

            @pl.loop(0, 4)
            def poisson(at):
                spectrum = turn(product(get("forward", at), work_ref[at]), turn_right)
                spectrum = turn(spectrum * weights, turn_right)
                work_ref[at] = product(get("inverse", at), spectrum)

            potential = [work_ref[at] for at in range(4)]
        field = []
        for at, quadrant in enumerate(unfold(potential)):
            term = quadrant * visit_ref[at]
            total = term[:, :lanes]
            for block in range(1, size):
                total = total + term[:, block * lanes : (block + 1) * lanes]
            if prior_ref is not None:
                total = total + prior_ref[at]
            if ends and step == len(sizes) - 1:
                field.append(total)
            else:
                field_ref[at] = total
        if not (ends and step == len(sizes) - 1):
            prior_ref = field_ref
    if ends:
        field = unfold(field)
        coefs = [product(get("project", at), field[at]) for at in range(4)]
        coefs = turn(jnp.concatenate(coefs, axis=0), turn_right)
        high, low = split(coefs.T)
        own_pick = pick[:, : out_ref.shape[1]]
        result = dot(high, own_pick) + dot(low, own_pick)
        out_ref[...] = result[: members * points]


def load_kernel(*refs):
    semaphores = refs[-1]
    count = (len(refs) - 1) // 2
    copies = [
        pltpu.make_async_copy(refs[at], refs[count + at], semaphores.at[at]) for at in range(count)
    ]
    for copy in copies:
        copy.start()
    for copy in copies:
        copy.wait()


def load(values):
    return pl.pallas_call(
        load_kernel,
        out_shape=[jax.ShapeDtypeStruct(value.shape, value.dtype) for value in values],
        in_specs=[pl.BlockSpec(memory_space=pl.ANY)] * len(values),
        out_specs=[pl.BlockSpec(memory_space=pltpu.VMEM)] * len(values),
        scratch_shapes=[pltpu.SemaphoreType.DMA((len(values),))],
        cost_estimate=pl.CostEstimate(flops=0, bytes_accessed=2**20, transcendentals=0),
        compiler_params=pltpu.CompilerParams(vmem_limit_bytes=16 * 2**20),
    )(*values)


def swap(value, axis, partner):
    count = lax.axis_size(axis)
    return lax.ppermute(value, axis, [(at, partner(at) % count) for at in range(count)])


def rest_of_ring(value, axis):
    count = lax.axis_size(axis)
    return [
        lax.ppermute(value, axis, [(at, (at + step) % count) for at in range(count)])
        for step in range(1, count)
    ]


def shards(stick_coefs, miller, stick_count):
    groups, members, points, per_owner = stick_coefs.shape
    owners = lax.axis_size("pw")
    batch = max(n for n in range(1, members + 1) if members % n == 0 and (n == 1 or n * points <= LANES))
    tables = build_tables(points, per_owner * owners, batch)
    shapes = {name: table.shape for name, table in tables.items()}
    small = tables["inverse"].shape[1] <= SMALL
    where = None
    if small:
        packed, where = pack_tables(tables)
        values = [jnp.asarray(packed)]
    else:
        values = [jnp.asarray(tables[name]) for name in TABLE_NAMES]
    own = stick_coefs.reshape(members * points, per_owner)
    others = rest_of_ring(own, "pw")
    if batch == members:
        (own,) = load([own])
    position = jnp.arange(per_owner, dtype=jnp.int32)[None]
    indices = jnp.where(position < stick_count[0], miller, -1).astype(jnp.float32)
    indices = jnp.concatenate([indices, jnp.zeros((6, per_owner), jnp.float32)], axis=0)
    indices = jnp.concatenate([indices] + rest_of_ring(indices, "pw"), axis=1)

    ring = lax.axis_size("band")
    coefs = jnp.stack([own] + others)
    mate = swap(coefs, "band", lambda at: at ^ 1)
    got = swap(jnp.stack([coefs, mate]), "band", lambda at: at + 1 if at & 1 else at - 1 + ring)

    lanes = tables["turn_right"].shape[0] // 2
    n_place, n_picked = tables["synth"].shape[1], tables["project"].shape[1]
    vmem = pl.BlockSpec(memory_space=pltpu.VMEM)
    grid_shape = jax.ShapeDtypeStruct((4, n_place, lanes), jnp.float32)

    pick_shape = jax.ShapeDtypeStruct((4 * n_picked, per_owner * owners), jnp.bfloat16)
    out_shape = jax.ShapeDtypeStruct((batch * points, per_owner), jnp.float32)

    def call(sizes, carried, groups_in, out_shape, begins=False, ends=False):
        wide = max(sizes) * lanes
        scratch = [
            pltpu.VMEM((4, n_place, wide), jnp.float32),
            pltpu.VMEM((4, 8 if small else n_place, wide), jnp.float32),
            pltpu.VMEM((4, n_picked, wide), jnp.float32),
        ]
        if begins and ends:
            scratch += [pltpu.VMEM(each.shape, each.dtype) for each in (pick_shape, grid_shape, grid_shape)]
        return pl.pallas_call(
            functools.partial(exchange_kernel, batch, points, sizes, begins, ends, shapes, where),
            out_shape=out_shape,
            in_specs=[vmem] * (len(carried) + len(groups_in) + len(values)),
            out_specs=jax.tree.map(lambda _: vmem, out_shape),
            scratch_shapes=scratch,
            cost_estimate=pl.CostEstimate(flops=5 * 10**9, bytes_accessed=4 * 2**20, transcendentals=0),
            compiler_params=pltpu.CompilerParams(vmem_limit_bytes=(24 if small else 50) * 2**20),
        )(*carried, *groups_in, *values)

    flag = jnp.ones((batch * points, per_owner), jnp.float32)
    if small and batch == members:
        pick, orbs, field, flag = call(
            (2,),
            (indices, flag),
            (coefs, mate),
            (pick_shape, grid_shape, grid_shape, jax.ShapeDtypeStruct(flag.shape, flag.dtype)),
            begins=True,
        )
        last = swap(jnp.where(flag > 0.0, got[0], 0.0), "band", lambda at: at ^ 1)
        field = call((2,), (pick, orbs, field), (got[0], got[1]), grid_shape)
        result = call((1,), (pick, orbs, field), (last,), out_shape, ends=True)
    else:
        last = swap(got[0], "band", lambda at: at ^ 1)

        def exchange(pieces):
            return call((2, 2, 1), (indices, flag), pieces, out_shape, begins=True, ends=True)

        def cut(piece):
            return piece.reshape(owners, -1, batch * points, per_owner).swapaxes(0, 1)

        pieces = (coefs, mate, got[0], got[1], last)
        if batch == members:
            result = exchange(pieces)
        else:
            result = lax.map(exchange, tuple(cut(piece) for piece in pieces))
    return result.reshape(groups, members, points, per_owner)


def solution(mesh):
    return jax.shard_map(
        shards,
        mesh=mesh,
        in_specs=(P("band", None, None, "pw"), P(None, "pw"), P("pw")),
        out_specs=P("band", None, None, "pw"),
        check_vma=False,
    )
```

```python
import functools
import math

import jax
import jax.numpy as jnp
import ml_dtypes
import numpy as np
from jax import lax
from jax.experimental import pallas as pl
from jax.experimental.pallas import tpu as pltpu
from jax.sharding import PartitionSpec as P

HALF = 2
kernel_scale = 4.0
screen_width = 16.0
LANES = 128
ROWS = 16
SMALL = 512
PARITIES = ("cc", "sc", "cs", "ss")


def round_up(value, unit):
    return -(-value // unit) * unit


def split_table(table):
    head = table.astype(np.float32).astype(ml_dtypes.bfloat16)
    rest = (table - head.astype(np.float64)).astype(np.float32).astype(ml_dtypes.bfloat16)
    return head, rest


@functools.lru_cache(maxsize=None)
def build_tables(points, sticks, members):
    signed = np.arange(points)
    signed = np.where(signed < points // 2, signed, signed - points)
    radius = signed[:, None] ** 2 + signed[None, :] ** 2
    limit = np.sort(radius.reshape(-1))[min(sticks, points * points) - 1]
    picked = sorted({(abs(b), abs(c)) for b in signed for c in signed if b * b + c * c <= limit})
    largest = max(b for b, _ in picked)
    grid = 4 * largest + 1 if 4 * largest + 1 < points else points

    def fold(value):
        value = value % points
        return min(value, points - value)

    pairs = set()
    for b1, c1 in picked:
        for b2, c2 in picked:
            for b in {fold(b1 + b2), fold(b1 - b2)}:
                for c in {fold(c1 + c2), fold(c1 - c2)}:
                    pairs.add((b, c))
    near = grid // 2 + 1

    def mirrored(value):
        return 2 * value % grid != 0

    def order(spots):
        return sorted(spots, key=lambda spot: (not mirrored(spot[0]), not mirrored(spot[1]), spot))

    pairs = order(pairs)
    place = order((y, z) for y in range(near) for z in range(near))
    place_weight = np.array([np.prod([1.0 if mirrored(v) else 0.5 for v in spot]) for spot in place])
    small = len(place) <= SMALL

    def wave(kind, freq, spot):
        angle = 2.0 * np.pi * ((freq[:, None] * spot[None, :]) % grid) / grid
        return np.cos(angle) if kind == "c" else np.sin(angle)

    def class_waves(kinds, freqs):
        freqs, spots = np.array(freqs), np.array(place)
        first = wave(kinds[0], freqs[:, 0], spots[:, 0])
        return first * wave(kinds[1], freqs[:, 1], spots[:, 1])

    def class_pairs(kinds):
        if not small:
            return pairs
        if kinds == "cs":
            return [(c, b) for b, c in class_pairs("sc")]
        return [p for p in pairs if all(kind == "c" or mirrored(v) for kind, v in zip(kinds, p))]

    def split_columns(table, rows, cols):
        full = np.zeros((rows, cols))
        full[: table.shape[0], : table.shape[1]] = table
        high, low = split_table(full)
        return np.concatenate([high, high, low], axis=1)

    n_place = round_up(len(place), ROWS)
    n_pairs = round_up(len(pairs), ROWS)
    n_picked = round_up(len(picked), ROWS)
    scale = points**-1.5
    by_parity = dict(synth=[], project=[], forward=[], inverse=[])
    for kinds in PARITIES:
        few = class_waves(kinds, picked)
        many = class_waves(kinds, class_pairs(kinds))
        rows, depth = n_pairs, n_place
        if small:
            rows = round_up(many.shape[0], ROWS)
            depth = round_up(1 + np.flatnonzero(np.abs(many).max(axis=0) > 1e-9)[-1], ROWS)
        few_back = -few * place_weight * scale * (points / grid) ** 2
        by_parity["synth"].append(split_columns(few.T * scale, n_place, n_picked))
        by_parity["project"].append(split_columns(few_back, n_picked, n_place))
        by_parity["forward"].append(split_columns((many * place_weight)[:, :depth], rows, depth))
        by_parity["inverse"].append(split_columns(many.T, n_place, rows))

    index = np.arange(points)
    angle = 2.0 * np.pi * ((index[:, None] * index[None, :]) % points) / points
    cas = np.cos(angle) + np.sin(angle)
    lanes = round_up(members * points, LANES)
    block = np.zeros((lanes, lanes))
    for member in range(members):
        at = member * points
        block[at : at + points, at : at + points] = cas
    high, low = split_table(block)
    turn_left = np.concatenate([high, high, low], axis=1)
    turn_right = np.block([[high, low], [high, low]])

    squares = signed.astype(np.float64) ** 2
    freqs = np.array(pairs)
    total = (freqs[:, 0] ** 2 + freqs[:, 1] ** 2)[:, None] + squares[None, :]
    scaled = total / screen_width
    safe = np.where(total > 0, scaled, 1.0)
    kernel = kernel_scale * np.where(total > 0, -np.expm1(-safe) / safe, 1.0)
    double = np.where(mirrored(freqs), 2.0, 1.0)
    kernel = kernel * (double[:, 0] * double[:, 1])[:, None]
    kernel = kernel * (points / grid) ** 2 / float(points**3)
    weights = np.zeros((n_pairs, lanes))
    for member in range(members):
        weights[: len(pairs), member * points : (member + 1) * points] = kernel

    codes = np.full((n_picked, LANES), -7.0)
    for at, (b, c) in enumerate(picked):
        codes[at, 0], codes[at, 1] = b, c
    tables = dict(
        turn_left=turn_left,
        turn_right=turn_right,
        weights=np.concatenate(split_table(weights), axis=1),
        codes=codes.astype(ml_dtypes.bfloat16),
    )
    for name, each in by_parity.items():
        if small:
            tables.update({name + str(at): table for at, table in enumerate(each)})
        else:
            tables[name] = np.stack(each)
    return tables, small


def pack_tables(tables):
    parities = [str(at) for at in range(len(PARITIES))]
    shelves = [("forward" + at,) for at in parities] + [("project" + at,) for at in parities]
    shelves += [("inverse" + at, "synth" + at) for at in parities]
    shelves.append(("turn_left", "turn_right", "weights", "codes"))
    where, row, width = {}, 0, 0
    for shelf in shelves:
        column = 0
        for name in shelf:
            where[name] = (row, column)
            column += round_up(tables[name].shape[1], LANES)
        row += round_up(max(tables[name].shape[0] for name in shelf), ROWS)
        width = max(width, column)
    packed = np.zeros((row, width), ml_dtypes.bfloat16)
    for name, (first, column) in where.items():
        rows, cols = tables[name].shape
        packed[first : first + rows, column : column + cols] = tables[name]
    return packed, where


def table_getter(shapes, refs, where):
    def get(name, at=None):
        if where is None:
            ref = refs[list(shapes).index(name)]
            return ref[...] if at is None else ref[at]
        name = name if at is None else name + str(at)
        (first, column), (rows, cols) = where[name], shapes[name]
        return refs[0][first : first + rows, column : column + cols]

    return get


def dot(left, right):
    return jnp.dot(left, right, preferred_element_type=jnp.float32)


def split(value):
    high = value.astype(jnp.bfloat16)
    low = (value - high.astype(jnp.float32)).astype(jnp.bfloat16)
    return high, low


def stacked(value):
    high, low = split(value)
    return jnp.concatenate([high, low, high], axis=0)


def product(table, value):
    return dot(table, stacked(value))


def pick_matrix(indices, codes, points):
    first, second = indices[0:1], indices[1:2]
    alive = first >= 0.0
    signed_first = jnp.where(first < points // 2, first, first - points)
    signed_second = jnp.where(second < points // 2, second, second - points)
    first_same = codes[:, 0:1] == jnp.where(alive, jnp.abs(signed_first), -1.0)
    one = jnp.where(first_same & (codes[:, 1:2] == jnp.abs(signed_second)), 1.0, 0.0)
    sign_first = jnp.where(signed_first < 0.0, -1.0, 1.0)
    sign_second = jnp.where(signed_second < 0.0, -1.0, 1.0)
    parts = [one, one * sign_first, one * sign_second, one * (sign_first * sign_second)]
    return jnp.concatenate(parts, axis=0).astype(jnp.bfloat16)


def unfold(parts):
    even, odd = parts[0] + parts[2], parts[1] + parts[3]
    even_less, odd_less = parts[0] - parts[2], parts[1] - parts[3]
    return [even + odd, even - odd, even_less + odd_less, even_less - odd_less]


def turn(value, turn_right):
    lanes = turn_right.shape[0] // 2
    outs = []
    for at in range(0, value.shape[1], lanes):
        high, low = split(value[:, at : at + lanes])
        out = dot(jnp.concatenate([high, low], axis=1), turn_right)
        outs.append(out[:, :lanes] + out[:, lanes:])
    return outs[0] if len(outs) == 1 else jnp.concatenate(outs, axis=1)


def each_part(small, body):
    if small:
        for at in range(4):
            body(at)
    else:
        pl.loop(0, 4)(body)


def synthesize(small, blocks, pick, get, coefs_ref, orbs_ref):
    turn_left = get("turn_left")
    fields = [dot(turn_left, stacked(block)) for block in blocks]
    field = fields[0] if len(fields) == 1 else jnp.concatenate(fields, axis=0)
    high, low = split(field)
    contract = (((1,), (1,)), ((), ()))
    coefs = lax.dot_general(pick, high, contract, preferred_element_type=jnp.float32)
    coefs = coefs + lax.dot_general(pick, low, contract, preferred_element_type=jnp.float32)
    rows = pick.shape[0] // 4
    for at in range(4):
        coefs_ref[at] = coefs[at * rows : (at + 1) * rows]

    def body(at):
        orbs_ref[at] = product(get("synth", at), coefs_ref[at])

    each_part(small, body)
    for at, quadrant in enumerate(unfold([orbs_ref[at] for at in range(4)])):
        orbs_ref[at] = quadrant


def exchange_kernel(members, points, owners, sizes, begins, ends, shapes, where, *refs):
    refs = list(refs)
    take = lambda count: [refs.pop(0) for _ in range(count)]
    prior_ref = None
    if begins:
        *indices_refs, flag_in_ref = take(owners + 1)
    else:
        pick_ref, own_ref, prior_ref = take(3)
    coef_refs = take(sum(sizes))
    get = table_getter(shapes, take(len(shapes) if where is None else 1), where)
    if ends:
        (out_ref,) = take(1)
    elif begins:
        pick_ref, own_ref, field_ref, flag_ref = take(4)
        flag_ref[...] = flag_in_ref[...]
    else:
        (field_ref,) = take(1)
    visit_all_ref, work_all_ref, coefs_all_ref = take(3)
    if begins and ends:
        pick_ref, own_ref, field_ref = take(3)
    if begins:
        pick_ref[...] = pick_matrix(jnp.concatenate([ref[...] for ref in indices_refs], axis=1), get("codes").astype(jnp.float32), points)
    pick, turn_right = pick_ref[...], get("turn_right")
    lanes = turn_right.shape[0] // 2
    pad = lanes - members * points
    small = where is not None

    def coefs_of(ref):
        block = jnp.concatenate([ref[at] for at in range(ref.shape[0])], axis=1)
        if pad:
            block = jnp.concatenate([block, jnp.zeros((pad, block.shape[1]), block.dtype)], axis=0)
        return block

    weight = get("weights").astype(jnp.float32)
    weight = weight[:, :lanes] + weight[:, lanes:]
    start = 0
    for step, size in enumerate(sizes):
        refs = [ref.at[:, :, : size * lanes] for ref in (visit_all_ref, work_all_ref, coefs_all_ref)]
        visit_ref, work_ref, coefs_ref = refs
        blocks = [coefs_of(ref) for ref in coef_refs[start : start + size]]
        start += size
        synthesize(small, blocks, pick, get, coefs_ref, visit_ref)
        if begins and step == 0:
            for at in range(4):
                own_ref[at] = visit_ref[at, :, :lanes]
        weights = jnp.concatenate([weight] * size, axis=1)
        density = []
        for at in range(4):
            density.append(jnp.concatenate([own_ref[at]] * size, axis=1) * visit_ref[at])
        density = unfold(density)
        if small:
            spectra = []
            for at in range(4):
                table = get("forward", at)
                spectra.append(product(table, density[at][: table.shape[1] // 3]))
            rows = [part.shape[0] for part in spectra]
            spectrum = turn(jnp.concatenate(spectra, axis=0), turn_right)
            spectrum = spectrum * jnp.concatenate([weights[:count] for count in rows], axis=0)
            spectrum = turn(spectrum, turn_right)
            potential = []
            for at in range(4):
                first = sum(rows[:at])
                potential.append(product(get("inverse", at), spectrum[first : first + rows[at]]))
        else:
            for at, part in enumerate(density):
                work_ref[at] = part

            @pl.loop(0, 4)
            def poisson(at):
                spectrum = turn(product(get("forward", at), work_ref[at]), turn_right)
                spectrum = turn(spectrum * weights, turn_right)
                work_ref[at] = product(get("inverse", at), spectrum)

            potential = [work_ref[at] for at in range(4)]
        field = []
        for at, quadrant in enumerate(unfold(potential)):
            term = quadrant * visit_ref[at]
            total = term[:, :lanes]
            for block in range(1, size):
                total = total + term[:, block * lanes : (block + 1) * lanes]
            if prior_ref is not None:
                total = total + prior_ref[at]
            if ends and step == len(sizes) - 1:
                field.append(total)
            else:
                field_ref[at] = total
        if not (ends and step == len(sizes) - 1):
            prior_ref = field_ref
    if ends:
        field = unfold(field)
        coefs = [product(get("project", at), field[at]) for at in range(4)]
        coefs = turn(jnp.concatenate(coefs, axis=0), turn_right)
        high, low = split(coefs.T)
        own_pick = pick[:, : out_ref.shape[1]]
        result = dot(high, own_pick) + dot(low, own_pick)
        out_ref[...] = result[: members * points]


def hold_kernel(*refs):
    semaphores = refs[-1]
    count = (len(refs) - 1) // 2
    copies = [
        pltpu.make_async_copy(refs[at], refs[count + at], semaphores.at[at]) for at in range(count)
    ]
    for copy in copies:
        copy.start()
    for copy in copies:
        copy.wait()


def hold(*values):
    return pl.pallas_call(
        hold_kernel,
        out_shape=[jax.ShapeDtypeStruct(value.shape, value.dtype) for value in values],
        in_specs=[pl.BlockSpec(memory_space=pl.ANY)] * len(values),
        out_specs=[pl.BlockSpec(memory_space=pltpu.VMEM)] * len(values),
        scratch_shapes=[pltpu.SemaphoreType.DMA((len(values),))],
        cost_estimate=pl.CostEstimate(flops=5 * 10**9, bytes_accessed=2**20, transcendentals=0),
        compiler_params=pltpu.CompilerParams(vmem_limit_bytes=16 * 2**20),
    )(*values)


def swap(value, axis, partner):
    count = lax.axis_size(axis)
    return lax.ppermute(value, axis, [(at, partner(at) % count) for at in range(count)])


def rest_of_ring(value, axis):
    count = lax.axis_size(axis)
    return [
        lax.ppermute(value, axis, [(at, (at + step) % count) for at in range(count)])
        for step in range(1, count)
    ]


def shards(stick_coefs, miller, stick_count):
    groups, members, points, per_owner = stick_coefs.shape
    owners = lax.axis_size("pw")
    batch = max(n for n in range(1, members + 1) if members % n == 0 and (n == 1 or n * points <= LANES))
    tables, small = build_tables(points, per_owner * owners, batch)
    shapes = {name: table.shape for name, table in tables.items()}
    where, held = None, list(tables.values())
    if small:
        packed, where = pack_tables(tables)
        held = [packed]
    values = [jnp.asarray(table) for table in held]
    own = stick_coefs.reshape(members * points, per_owner)
    others = rest_of_ring(own, "pw")
    position = jnp.arange(per_owner, dtype=jnp.int32)[None]
    indices = jnp.where(position < stick_count[0], miller, -1).astype(jnp.float32)
    indices = jnp.concatenate([indices, jnp.zeros((6, per_owner), jnp.float32)], axis=0)
    other_indices = rest_of_ring(indices, "pw")
    own, indices = hold(own, indices)
    indices = [indices] + other_indices

    ring = lax.axis_size("band")
    coefs = jnp.stack([own] + others)
    mate = swap(coefs, "band", lambda at: at ^ 1)
    got = swap(jnp.stack([coefs, mate]), "band", lambda at: at + 1 if at & 1 else at - 1 + ring)

    lanes = tables["turn_right"].shape[0] // 2
    n_place, n_picked = shapes["synth0" if small else "synth"][-2], shapes["codes"][0]
    vmem = pl.BlockSpec(memory_space=pltpu.VMEM)
    grid_shape = jax.ShapeDtypeStruct((4, n_place, lanes), jnp.float32)

    pick_shape = jax.ShapeDtypeStruct((4 * n_picked, per_owner * owners), jnp.bfloat16)
    out_shape = jax.ShapeDtypeStruct((batch * points, per_owner), jnp.float32)

    def call(sizes, carried, groups_in, out_shape, begins=False, ends=False):
        wide = max(sizes) * lanes
        scratch = [
            pltpu.VMEM((4, n_place, wide), jnp.float32),
            pltpu.VMEM((4, 8 if small else n_place, wide), jnp.float32),
            pltpu.VMEM((4, n_picked, wide), jnp.float32),
        ]
        if begins and ends:
            scratch += [pltpu.VMEM(each.shape, each.dtype) for each in (pick_shape, grid_shape, grid_shape)]
        return pl.pallas_call(
            functools.partial(exchange_kernel, batch, points, owners, sizes, begins, ends, shapes, where),
            out_shape=out_shape,
            in_specs=[vmem] * (len(carried) + len(groups_in) + len(values)),
            out_specs=jax.tree.map(lambda _: vmem, out_shape),
            scratch_shapes=scratch,
            cost_estimate=pl.CostEstimate(flops=5 * 10**9, bytes_accessed=4 * 2**20, transcendentals=0),
            compiler_params=pltpu.CompilerParams(vmem_limit_bytes=(24 if small else 50) * 2**20),
        )(*carried, *groups_in, *values)

    flag = jnp.ones((batch * points, per_owner), jnp.float32)
    if small and batch == members:
        pick, orbs, field, flag = call(
            (2,),
            (*indices, flag),
            (coefs, mate),
            (pick_shape, grid_shape, grid_shape, jax.ShapeDtypeStruct(flag.shape, flag.dtype)),
            begins=True,
        )
        last = swap(jnp.where(flag > 0.0, got[0], 0.0), "band", lambda at: at ^ 1)
        field = call((2,), (pick, orbs, field), (got[0], got[1]), grid_shape)
        result = call((1,), (pick, orbs, field), (last,), out_shape, ends=True)
    else:
        last = swap(got[0], "band", lambda at: at ^ 1)

        def exchange(pieces):
            return call((2, 2, 1), (*indices, flag), pieces, out_shape, begins=True, ends=True)

        def cut(piece):
            return piece.reshape(owners, -1, batch * points, per_owner).swapaxes(0, 1)

        pieces = (coefs, mate, got[0], got[1], last)
        if batch == members:
            result = exchange(pieces)
        else:
            result = lax.map(exchange, tuple(cut(piece) for piece in pieces))
    return result.reshape(groups, members, points, per_owner)


def solution(mesh):
    return jax.shard_map(
        shards,
        mesh=mesh,
        in_specs=(P("band", None, None, "pw"), P(None, "pw"), P("pw")),
        out_specs=P("band", None, None, "pw"),
        check_vma=False,
    )
```

```python
import functools
import math

import jax
import jax.numpy as jnp
import ml_dtypes
import numpy as np
from jax import lax
from jax.experimental import pallas as pl
from jax.experimental.pallas import tpu as pltpu
from jax.sharding import PartitionSpec as P

HALF = 2
kernel_scale = 4.0
screen_width = 16.0
LANES = 128
ROWS = 16
SMALL = 512
PARITIES = ("cc", "sc", "cs", "ss")


def round_up(value, unit):
    return -(-value // unit) * unit


def split_table(table):
    head = table.astype(np.float32).astype(ml_dtypes.bfloat16)
    rest = (table - head.astype(np.float64)).astype(np.float32).astype(ml_dtypes.bfloat16)
    return head, rest


@functools.lru_cache(maxsize=None)
def build_tables(points, sticks, members):
    signed = np.arange(points)
    signed = np.where(signed < points // 2, signed, signed - points)
    radius = signed[:, None] ** 2 + signed[None, :] ** 2
    limit = np.sort(radius.reshape(-1))[min(sticks, points * points) - 1]
    picked = sorted({(abs(b), abs(c)) for b in signed for c in signed if b * b + c * c <= limit})
    largest = max(b for b, _ in picked)
    grid = 4 * largest + 1 if 4 * largest + 1 < points else points

    def fold(value):
        value = value % points
        return min(value, points - value)

    pairs = set()
    for b1, c1 in picked:
        for b2, c2 in picked:
            for b in {fold(b1 + b2), fold(b1 - b2)}:
                for c in {fold(c1 + c2), fold(c1 - c2)}:
                    pairs.add((b, c))
    near = grid // 2 + 1

    def mirrored(value):
        return 2 * value % grid != 0

    def order(spots):
        return sorted(spots, key=lambda spot: (not mirrored(spot[0]), not mirrored(spot[1]), spot))

    pairs = order(pairs)
    place = order((y, z) for y in range(near) for z in range(near))
    place_weight = np.array([np.prod([1.0 if mirrored(v) else 0.5 for v in spot]) for spot in place])
    small = len(place) <= SMALL

    def wave(kind, freq, spot):
        angle = 2.0 * np.pi * ((freq[:, None] * spot[None, :]) % grid) / grid
        return np.cos(angle) if kind == "c" else np.sin(angle)

    def class_waves(kinds, freqs):
        freqs, spots = np.array(freqs), np.array(place)
        first = wave(kinds[0], freqs[:, 0], spots[:, 0])
        return first * wave(kinds[1], freqs[:, 1], spots[:, 1])

    def class_pairs(kinds):
        if not small:
            return pairs
        if kinds == "cs":
            return [(c, b) for b, c in class_pairs("sc")]
        return [p for p in pairs if all(kind == "c" or mirrored(v) for kind, v in zip(kinds, p))]

    def split_columns(table, rows, cols):
        full = np.zeros((rows, cols))
        full[: table.shape[0], : table.shape[1]] = table
        high, low = split_table(full)
        return np.concatenate([high, high, low], axis=1)

    n_place = round_up(len(place), ROWS)
    n_pairs = round_up(len(pairs), ROWS)
    n_picked = round_up(len(picked), ROWS)
    scale = points**-1.5
    by_parity = dict(synth=[], project=[], forward=[], inverse=[])
    for kinds in PARITIES:
        few = class_waves(kinds, picked)
        many = class_waves(kinds, class_pairs(kinds))
        rows, depth = n_pairs, n_place
        if small:
            rows = round_up(many.shape[0], ROWS)
            depth = round_up(1 + np.flatnonzero(np.abs(many).max(axis=0) > 1e-9)[-1], ROWS)
        few_back = -few * place_weight * scale * (points / grid) ** 2
        by_parity["synth"].append(split_columns(few.T * scale, n_place, n_picked))
        by_parity["project"].append(split_columns(few_back, n_picked, n_place))
        by_parity["forward"].append(split_columns((many * place_weight)[:, :depth], rows, depth))
        by_parity["inverse"].append(split_columns(many.T, n_place, rows))

    index = np.arange(points)
    angle = 2.0 * np.pi * ((index[:, None] * index[None, :]) % points) / points
    cas = np.cos(angle) + np.sin(angle)
    lanes = round_up(members * points, LANES)
    block = np.zeros((lanes, lanes))
    for member in range(members):
        at = member * points
        block[at : at + points, at : at + points] = cas
    high, low = split_table(block)
    turn_left = np.concatenate([high, high, low], axis=1)
    turn_right = np.block([[high, low], [high, low]])

    squares = signed.astype(np.float64) ** 2
    freqs = np.array(pairs)
    total = (freqs[:, 0] ** 2 + freqs[:, 1] ** 2)[:, None] + squares[None, :]
    scaled = total / screen_width
    safe = np.where(total > 0, scaled, 1.0)
    kernel = kernel_scale * np.where(total > 0, -np.expm1(-safe) / safe, 1.0)
    double = np.where(mirrored(freqs), 2.0, 1.0)
    kernel = kernel * (double[:, 0] * double[:, 1])[:, None]
    kernel = kernel * (points / grid) ** 2 / float(points**3)
    weights = np.zeros((n_pairs, lanes))
    for member in range(members):
        weights[: len(pairs), member * points : (member + 1) * points] = kernel

    codes = np.full((n_picked, LANES), -7.0)
    for at, (b, c) in enumerate(picked):
        codes[at, 0], codes[at, 1] = b, c
    tables = dict(
        turn_left=turn_left,
        turn_right=turn_right,
        weights=np.concatenate(split_table(weights), axis=1),
        codes=codes.astype(ml_dtypes.bfloat16),
    )
    for name, each in by_parity.items():
        if small:
            tables.update({name + str(at): table for at, table in enumerate(each)})
        else:
            tables[name] = np.stack(each)
    return tables, small


def pack_tables(tables):
    parities = [str(at) for at in range(len(PARITIES))]
    shelves = [("forward" + at,) for at in parities] + [("project" + at,) for at in parities]
    shelves += [("inverse" + at, "synth" + at) for at in parities]
    shelves.append(("turn_left", "turn_right", "weights", "codes"))
    where, row, width = {}, 0, 0
    for shelf in shelves:
        column = 0
        for name in shelf:
            where[name] = (row, column)
            column += round_up(tables[name].shape[1], LANES)
        row += round_up(max(tables[name].shape[0] for name in shelf), ROWS)
        width = max(width, column)
    packed = np.zeros((row, width), ml_dtypes.bfloat16)
    for name, (first, column) in where.items():
        rows, cols = tables[name].shape
        packed[first : first + rows, column : column + cols] = tables[name]
    return packed, where


def table_getter(shapes, refs, where):
    def get(name, at=None):
        if where is None:
            ref = refs[list(shapes).index(name)]
            return ref[...] if at is None else ref[at]
        name = name if at is None else name + str(at)
        (first, column), (rows, cols) = where[name], shapes[name]
        return refs[0][first : first + rows, column : column + cols]

    return get


def dot(left, right):
    return jnp.dot(left, right, preferred_element_type=jnp.float32)


def split(value):
    high = value.astype(jnp.bfloat16)
    low = (value - high.astype(jnp.float32)).astype(jnp.bfloat16)
    return high, low


def stacked(value):
    high, low = split(value)
    return jnp.concatenate([high, low, high], axis=0)


def product(table, value):
    depth, lanes = value.shape
    if lanes > LANES or depth <= LANES:
        return dot(table, stacked(value))
    high, low = split(value)
    out = dot(table[:, :depth], jnp.concatenate([high, low], axis=1))
    return out[:, :lanes] + out[:, lanes:] + dot(table[:, 2 * depth :], high)


def pick_matrix(indices, codes, points):
    first, second = indices[0:1], indices[1:2]
    alive = first >= 0.0
    signed_first = jnp.where(first < points // 2, first, first - points)
    signed_second = jnp.where(second < points // 2, second, second - points)
    first_same = codes[:, 0:1] == jnp.where(alive, jnp.abs(signed_first), -1.0)
    one = jnp.where(first_same & (codes[:, 1:2] == jnp.abs(signed_second)), 1.0, 0.0)
    sign_first = jnp.where(signed_first < 0.0, -1.0, 1.0)
    sign_second = jnp.where(signed_second < 0.0, -1.0, 1.0)
    parts = [one, one * sign_first, one * sign_second, one * (sign_first * sign_second)]
    return jnp.concatenate(parts, axis=0).astype(jnp.bfloat16)


def unfold(parts):
    even, odd = parts[0] + parts[2], parts[1] + parts[3]
    even_less, odd_less = parts[0] - parts[2], parts[1] - parts[3]
    return [even + odd, even - odd, even_less + odd_less, even_less - odd_less]


def turn(value, turn_right):
    lanes = turn_right.shape[0] // 2
    outs = []
    for at in range(0, value.shape[1], lanes):
        high, low = split(value[:, at : at + lanes])
        out = dot(jnp.concatenate([high, low], axis=1), turn_right)
        outs.append(out[:, :lanes] + out[:, lanes:])
    return outs[0] if len(outs) == 1 else jnp.concatenate(outs, axis=1)


def each_part(small, body):
    if small:
        for at in range(4):
            body(at)
    else:
        pl.loop(0, 4)(body)


def synthesize(small, blocks, pick, get, coefs_ref, orbs_ref):
    turn_left = get("turn_left")
    fields = [dot(turn_left, stacked(block)) for block in blocks]
    field = fields[0] if len(fields) == 1 else jnp.concatenate(fields, axis=0)
    high, low = split(field)
    contract = (((1,), (1,)), ((), ()))
    coefs = lax.dot_general(pick, high, contract, preferred_element_type=jnp.float32)
    coefs = coefs + lax.dot_general(pick, low, contract, preferred_element_type=jnp.float32)
    rows = pick.shape[0] // 4
    for at in range(4):
        coefs_ref[at] = coefs[at * rows : (at + 1) * rows]

    def body(at):
        orbs_ref[at] = product(get("synth", at), coefs_ref[at])

    each_part(small, body)
    for at, quadrant in enumerate(unfold([orbs_ref[at] for at in range(4)])):
        orbs_ref[at] = quadrant


def read_coefs(ref, lanes):
    block = jnp.concatenate([ref[at] for at in range(ref.shape[0])], axis=1)
    pad = lanes - block.shape[0]
    if pad:
        block = jnp.concatenate([block, jnp.zeros((pad, block.shape[1]), block.dtype)], axis=0)
    return block


def orbitals_kernel(count, shapes, where, pick_ref, *refs):
    get = table_getter(shapes, refs[count:-count - 2], where)
    out_refs, (all_ref, coefs_ref) = refs[-count - 2 : -2], refs[-2:]
    lanes = get("turn_right").shape[0] // 2
    blocks = [read_coefs(ref, lanes) for ref in refs[:count]]
    synthesize(True, blocks, pick_ref[...], get, coefs_ref, all_ref)
    for at in range(4):
        for block, out_ref in enumerate(out_refs):
            out_ref[at] = all_ref[at, :, block * lanes : (block + 1) * lanes]


def exchange_kernel(members, points, owners, sizes, begins, ends, ready, shapes, where, *refs):
    refs = list(refs)
    take = lambda count: [refs.pop(0) for _ in range(count)]
    prior_ref = None
    if begins:
        indices_refs = take(owners)
    else:
        pick_ref, own_ref, prior_ref = take(3)
    coef_refs = take(sum(sizes))
    get = table_getter(shapes, take(len(shapes) if where is None else 1), where)
    if ends:
        (out_ref,) = take(1)
    elif begins:
        pick_ref, own_ref, field_ref = take(3)
    else:
        (field_ref,) = take(1)
    visit_all_ref, work_all_ref, coefs_all_ref = take(3)
    if begins and ends:
        pick_ref, own_ref, field_ref = take(3)
    if begins:
        pick_ref[...] = pick_matrix(jnp.concatenate([ref[...] for ref in indices_refs], axis=1), get("codes").astype(jnp.float32), points)
    pick, turn_right = pick_ref[...], get("turn_right")
    lanes = turn_right.shape[0] // 2
    small = where is not None
    weight = get("weights").astype(jnp.float32)
    weight = weight[:, :lanes] + weight[:, lanes:]
    start = 0
    for step, size in enumerate(sizes):
        refs = [ref.at[:, :, : size * lanes] for ref in (visit_all_ref, work_all_ref, coefs_all_ref)]
        visit_ref, work_ref, coefs_ref = refs
        group_refs = coef_refs[start : start + size]
        start += size
        if ready:
            visit = [jnp.concatenate([ref[at] for ref in group_refs], axis=1) for at in range(4)]
        else:
            blocks = [read_coefs(ref, lanes) for ref in group_refs]
            synthesize(small, blocks, pick, get, coefs_ref, visit_ref)
            visit = [visit_ref[at] for at in range(4)]
        if begins and step == 0:
            for at in range(4):
                own_ref[at] = visit_ref[at, :, :lanes]
        weights = jnp.concatenate([weight] * size, axis=1)
        density = []
        for at in range(4):
            density.append(jnp.concatenate([own_ref[at]] * size, axis=1) * visit[at])
        density = unfold(density)
        if small:
            spectra = []
            for at in range(4):
                table = get("forward", at)
                spectra.append(product(table, density[at][: table.shape[1] // 3]))
            rows = [part.shape[0] for part in spectra]
            spectrum = turn(jnp.concatenate(spectra, axis=0), turn_right)
            spectrum = spectrum * jnp.concatenate([weights[:count] for count in rows], axis=0)
            spectrum = turn(spectrum, turn_right)
            potential = []
            for at in range(4):
                first = sum(rows[:at])
                potential.append(product(get("inverse", at), spectrum[first : first + rows[at]]))
        else:
            for at, part in enumerate(density):
                work_ref[at] = part

            @pl.loop(0, 4)
            def poisson(at):
                spectrum = turn(product(get("forward", at), work_ref[at]), turn_right)
                spectrum = turn(spectrum * weights, turn_right)
                work_ref[at] = product(get("inverse", at), spectrum)

            potential = [work_ref[at] for at in range(4)]
        field = []
        for at, quadrant in enumerate(unfold(potential)):
            term = quadrant * visit[at]
            total = term[:, :lanes]
            for block in range(1, size):
                total = total + term[:, block * lanes : (block + 1) * lanes]
            if prior_ref is not None:
                total = total + prior_ref[at]
            if ends and step == len(sizes) - 1:
                field.append(total)
            else:
                field_ref[at] = total
        if not (ends and step == len(sizes) - 1):
            prior_ref = field_ref
    if ends:
        field = unfold(field)
        coefs = [product(get("project", at), field[at]) for at in range(4)]
        coefs = turn(jnp.concatenate(coefs, axis=0), turn_right)
        high, low = split(coefs.T)
        own_pick = pick[:, : out_ref.shape[1]]
        result = dot(high, own_pick) + dot(low, own_pick)
        out_ref[...] = result[: members * points]


def hold_kernel(*refs):
    semaphores = refs[-1]
    count = (len(refs) - 1) // 2
    copies = [
        pltpu.make_async_copy(refs[at], refs[count + at], semaphores.at[at]) for at in range(count)
    ]
    for copy in copies:
        copy.start()
    for copy in copies:
        copy.wait()


def hold(*values):
    return pl.pallas_call(
        hold_kernel,
        out_shape=[jax.ShapeDtypeStruct(value.shape, value.dtype) for value in values],
        in_specs=[pl.BlockSpec(memory_space=pl.ANY)] * len(values),
        out_specs=[pl.BlockSpec(memory_space=pltpu.VMEM)] * len(values),
        scratch_shapes=[pltpu.SemaphoreType.DMA((len(values),))],
        cost_estimate=pl.CostEstimate(flops=5 * 10**9, bytes_accessed=2**20, transcendentals=0),
        compiler_params=pltpu.CompilerParams(vmem_limit_bytes=16 * 2**20),
    )(*values)


def swap(value, axis, partner):
    count = lax.axis_size(axis)
    return lax.ppermute(value, axis, [(at, partner(at) % count) for at in range(count)])


def rest_of_ring(value, axis):
    count = lax.axis_size(axis)
    return [
        lax.ppermute(value, axis, [(at, (at + step) % count) for at in range(count)])
        for step in range(1, count)
    ]


def shards(stick_coefs, miller, stick_count):
    groups, members, points, per_owner = stick_coefs.shape
    owners = lax.axis_size("pw")
    batch = max(n for n in range(1, members + 1) if members % n == 0 and (n == 1 or n * points <= LANES))
    tables, small = build_tables(points, per_owner * owners, batch)
    shapes = {name: table.shape for name, table in tables.items()}
    where, held = None, list(tables.values())
    if small:
        packed, where = pack_tables(tables)
        held = [packed]
    values = [jnp.asarray(table) for table in held]
    own = stick_coefs.reshape(members * points, per_owner)
    others = rest_of_ring(own, "pw")
    position = jnp.arange(per_owner, dtype=jnp.int32)[None]
    indices = jnp.where(position < stick_count[0], miller, -1).astype(jnp.float32)
    indices = jnp.concatenate([indices, jnp.zeros((6, per_owner), jnp.float32)], axis=0)
    other_indices = rest_of_ring(indices, "pw")
    own, indices = hold(own, indices)
    indices = [indices] + other_indices

    ring = lax.axis_size("band")
    coefs = jnp.stack([own] + others)
    mate = swap(coefs, "band", lambda at: at ^ 1)
    got = swap(jnp.stack([coefs, mate]), "band", lambda at: at + 1 if at & 1 else at - 1 + ring)

    lanes = tables["turn_right"].shape[0] // 2
    n_place, n_picked = shapes["synth0" if small else "synth"][-2], shapes["codes"][0]
    vmem = pl.BlockSpec(memory_space=pltpu.VMEM)
    grid_shape = jax.ShapeDtypeStruct((4, n_place, lanes), jnp.float32)

    pick_shape = jax.ShapeDtypeStruct((4 * n_picked, per_owner * owners), jnp.bfloat16)
    out_shape = jax.ShapeDtypeStruct((batch * points, per_owner), jnp.float32)

    def call(sizes, carried, groups_in, out_shape, begins=False, ends=False, ready=False):
        wide = max(sizes) * lanes
        scratch = [
            pltpu.VMEM((4, n_place, wide), jnp.float32),
            pltpu.VMEM((4, 8 if small else n_place, wide), jnp.float32),
            pltpu.VMEM((4, n_picked, wide), jnp.float32),
        ]
        if begins and ends:
            scratch += [pltpu.VMEM(each.shape, each.dtype) for each in (pick_shape, grid_shape, grid_shape)]
        return pl.pallas_call(
            functools.partial(
                exchange_kernel, batch, points, owners, sizes, begins, ends, ready, shapes, where
            ),
            out_shape=out_shape,
            in_specs=[vmem] * (len(carried) + len(groups_in) + len(values)),
            out_specs=jax.tree.map(lambda _: vmem, out_shape),
            scratch_shapes=scratch,
            cost_estimate=pl.CostEstimate(flops=5 * 10**9, bytes_accessed=4 * 2**20, transcendentals=0),
            compiler_params=pltpu.CompilerParams(vmem_limit_bytes=(24 if small else 50) * 2**20),
        )(*carried, *groups_in, *values)

    def orbitals_of(pick, groups_in):
        count = len(groups_in)
        return pl.pallas_call(
            functools.partial(orbitals_kernel, count, shapes, where),
            out_shape=[grid_shape] * count,
            in_specs=[vmem] * (1 + count + len(values)),
            out_specs=[vmem] * count,
            scratch_shapes=[
                pltpu.VMEM((4, n_place, count * lanes), jnp.float32),
                pltpu.VMEM((4, n_picked, count * lanes), jnp.float32),
            ],
            cost_estimate=pl.CostEstimate(flops=10**9, bytes_accessed=2**20, transcendentals=0),
            compiler_params=pltpu.CompilerParams(vmem_limit_bytes=24 * 2**20),
        )(pick, *groups_in, *values)

    if small and batch == members:
        pick, orbs, field = call(
            (2,), indices, (coefs, mate), (pick_shape, grid_shape, grid_shape), begins=True
        )
        near, far = orbitals_of(pick, (got[0], got[1]))
        last = swap(near, "band", lambda at: at ^ 1)
        field = call((2,), (pick, orbs, field), (near, far), grid_shape, ready=True)
        result = call((1,), (pick, orbs, field), (last,), out_shape, ends=True, ready=True)
    else:
        last = swap(got[0], "band", lambda at: at ^ 1)

        def exchange(pieces):
            return call((2, 2, 1), indices, pieces, out_shape, begins=True, ends=True)

        def cut(piece):
            return piece.reshape(owners, -1, batch * points, per_owner).swapaxes(0, 1)

        pieces = (coefs, mate, got[0], got[1], last)
        if batch == members:
            result = exchange(pieces)
        else:
            result = lax.map(exchange, tuple(cut(piece) for piece in pieces))
    return result.reshape(groups, members, points, per_owner)


def solution(mesh):
    return jax.shard_map(
        shards,
        mesh=mesh,
        in_specs=(P("band", None, None, "pw"), P(None, "pw"), P("pw")),
        out_specs=P("band", None, None, "pw"),
        check_vma=False,
    )
```

```python
import functools
import math

import jax
import jax.numpy as jnp
import ml_dtypes
import numpy as np
from jax import lax
from jax.experimental import pallas as pl
from jax.experimental.pallas import tpu as pltpu
from jax.sharding import PartitionSpec as P

HALF = 2
kernel_scale = 4.0
screen_width = 16.0
LANES = 128
ROWS = 16
SMALL = 512
PARITIES = ("cc", "sc", "cs", "ss")


def round_up(value, unit):
    return -(-value // unit) * unit


def split_table(table):
    head = table.astype(np.float32).astype(ml_dtypes.bfloat16)
    rest = (table - head.astype(np.float64)).astype(np.float32).astype(ml_dtypes.bfloat16)
    return head, rest


@functools.lru_cache(maxsize=None)
def build_tables(points, sticks, members):
    signed = np.arange(points)
    signed = np.where(signed < points // 2, signed, signed - points)
    radius = signed[:, None] ** 2 + signed[None, :] ** 2
    limit = np.sort(radius.reshape(-1))[min(sticks, points * points) - 1]
    picked = sorted({(abs(b), abs(c)) for b in signed for c in signed if b * b + c * c <= limit})
    largest = max(b for b, _ in picked)
    grid = 4 * largest + 1 if 4 * largest + 1 < points else points

    def fold(value):
        value = value % points
        return min(value, points - value)

    pairs = set()
    for b1, c1 in picked:
        for b2, c2 in picked:
            for b in {fold(b1 + b2), fold(b1 - b2)}:
                for c in {fold(c1 + c2), fold(c1 - c2)}:
                    pairs.add((b, c))
    near = grid // 2 + 1

    def mirrored(value):
        return 2 * value % grid != 0

    def order(spots):
        return sorted(spots, key=lambda spot: (not mirrored(spot[0]), not mirrored(spot[1]), spot))

    pairs = order(pairs)
    place = order((y, z) for y in range(near) for z in range(near))
    place_weight = np.array([np.prod([1.0 if mirrored(v) else 0.5 for v in spot]) for spot in place])
    small = len(place) <= SMALL

    def wave(kind, freq, spot):
        angle = 2.0 * np.pi * ((freq[:, None] * spot[None, :]) % grid) / grid
        return np.cos(angle) if kind == "c" else np.sin(angle)

    def class_waves(kinds, freqs):
        freqs, spots = np.array(freqs), np.array(place)
        first = wave(kinds[0], freqs[:, 0], spots[:, 0])
        return first * wave(kinds[1], freqs[:, 1], spots[:, 1])

    def class_pairs(kinds):
        if not small:
            return pairs
        if kinds == "cs":
            return [(c, b) for b, c in class_pairs("sc")]
        return [p for p in pairs if all(kind == "c" or mirrored(v) for kind, v in zip(kinds, p))]

    def split_columns(table, rows, cols):
        full = np.zeros((rows, cols))
        full[: table.shape[0], : table.shape[1]] = table
        high, low = split_table(full)
        return np.concatenate([high, high, low], axis=1)

    n_place = round_up(len(place), ROWS)
    n_pairs = round_up(len(pairs), ROWS)
    n_picked = round_up(len(picked), ROWS)
    scale = points**-1.5
    by_parity = dict(synth=[], project=[], forward=[], inverse=[])
    for kinds in PARITIES:
        few = class_waves(kinds, picked)
        many = class_waves(kinds, class_pairs(kinds))
        rows, depth = n_pairs, n_place
        if small:
            rows = round_up(many.shape[0], ROWS)
            depth = round_up(1 + np.flatnonzero(np.abs(many).max(axis=0) > 1e-9)[-1], ROWS)
        few_back = -few * place_weight * scale * (points / grid) ** 2
        by_parity["synth"].append(split_columns(few.T * scale, n_place, n_picked))
        by_parity["project"].append(split_columns(few_back, n_picked, n_place))
        by_parity["forward"].append(split_columns((many * place_weight)[:, :depth], rows, depth))
        by_parity["inverse"].append(split_columns(many.T, n_place, rows))

    index = np.arange(points)
    angle = 2.0 * np.pi * ((index[:, None] * index[None, :]) % points) / points
    cas = np.cos(angle) + np.sin(angle)
    lanes = round_up(members * points, LANES)
    block = np.zeros((lanes, lanes))
    for member in range(members):
        at = member * points
        block[at : at + points, at : at + points] = cas
    high, low = split_table(block)
    turn_left = np.concatenate([high, high, low], axis=1)
    turn_right = np.block([[high, low], [high, low]])

    squares = signed.astype(np.float64) ** 2
    freqs = np.array(pairs)
    total = (freqs[:, 0] ** 2 + freqs[:, 1] ** 2)[:, None] + squares[None, :]
    scaled = total / screen_width
    safe = np.where(total > 0, scaled, 1.0)
    kernel = kernel_scale * np.where(total > 0, -np.expm1(-safe) / safe, 1.0)
    double = np.where(mirrored(freqs), 2.0, 1.0)
    kernel = kernel * (double[:, 0] * double[:, 1])[:, None]
    kernel = kernel * (points / grid) ** 2 / float(points**3)
    weights = np.zeros((n_pairs, lanes))
    for member in range(members):
        weights[: len(pairs), member * points : (member + 1) * points] = kernel

    codes = np.full((n_picked, LANES), -7.0)
    for at, (b, c) in enumerate(picked):
        codes[at, 0], codes[at, 1] = b, c
    tables = dict(
        turn_left=turn_left,
        turn_right=turn_right,
        weights=np.concatenate(split_table(weights), axis=1),
        codes=codes.astype(ml_dtypes.bfloat16),
    )
    for name, each in by_parity.items():
        if small:
            tables.update({name + str(at): table for at, table in enumerate(each)})
        else:
            tables[name] = np.stack(each)
    return tables, small


def pack_tables(tables):
    parities = [str(at) for at in range(len(PARITIES))]
    shelves = [("forward" + at,) for at in parities] + [("project" + at,) for at in parities]
    shelves += [("inverse" + at, "synth" + at) for at in parities]
    shelves.append(("turn_left", "turn_right", "weights", "codes"))
    where, row, width = {}, 0, 0
    for shelf in shelves:
        column = 0
        for name in shelf:
            where[name] = (row, column)
            column += round_up(tables[name].shape[1], LANES)
        row += round_up(max(tables[name].shape[0] for name in shelf), ROWS)
        width = max(width, column)
    packed = np.zeros((row, width), ml_dtypes.bfloat16)
    for name, (first, column) in where.items():
        rows, cols = tables[name].shape
        packed[first : first + rows, column : column + cols] = tables[name]
    return packed, where


def table_getter(shapes, refs, where):
    def get(name, at=None):
        if where is None:
            ref = refs[list(shapes).index(name)]
            return ref[...] if at is None else ref[at]
        name = name if at is None else name + str(at)
        (first, column), (rows, cols) = where[name], shapes[name]
        return refs[0][first : first + rows, column : column + cols]

    return get


def dot(left, right):
    return jnp.dot(left, right, preferred_element_type=jnp.float32)


def split(value):
    high = value.astype(jnp.bfloat16)
    low = (value - high.astype(jnp.float32)).astype(jnp.bfloat16)
    return high, low


def stacked(value):
    high, low = split(value)
    return jnp.concatenate([high, low, high], axis=0)


def product(table, value):
    depth, lanes = value.shape
    if lanes > LANES or depth <= LANES:
        return dot(table, stacked(value))
    high, low = split(value)
    out = dot(table[:, :depth], jnp.concatenate([high, low], axis=1))
    return out[:, :lanes] + out[:, lanes:] + dot(table[:, 2 * depth :], high)


def pick_matrix(indices, codes, points):
    first, second = indices[0:1], indices[1:2]
    alive = first >= 0.0
    signed_first = jnp.where(first < points // 2, first, first - points)
    signed_second = jnp.where(second < points // 2, second, second - points)
    first_same = codes[:, 0:1] == jnp.where(alive, jnp.abs(signed_first), -1.0)
    one = jnp.where(first_same & (codes[:, 1:2] == jnp.abs(signed_second)), 1.0, 0.0)
    sign_first = jnp.where(signed_first < 0.0, -1.0, 1.0)
    sign_second = jnp.where(signed_second < 0.0, -1.0, 1.0)
    parts = [one, one * sign_first, one * sign_second, one * (sign_first * sign_second)]
    return jnp.concatenate(parts, axis=0).astype(jnp.bfloat16)


def unfold(parts):
    even, odd = parts[0] + parts[2], parts[1] + parts[3]
    even_less, odd_less = parts[0] - parts[2], parts[1] - parts[3]
    return [even + odd, even - odd, even_less + odd_less, even_less - odd_less]


def turn(value, turn_right):
    lanes = turn_right.shape[0] // 2
    outs = []
    for at in range(0, value.shape[1], lanes):
        high, low = split(value[:, at : at + lanes])
        out = dot(jnp.concatenate([high, low], axis=1), turn_right)
        outs.append(out[:, :lanes] + out[:, lanes:])
    return outs[0] if len(outs) == 1 else jnp.concatenate(outs, axis=1)


def each_part(small, body):
    if small:
        for at in range(4):
            body(at)
    else:
        pl.loop(0, 4)(body)


def synthesize(small, blocks, pick, get, coefs_ref, orbs_ref):
    turn_left = get("turn_left")
    fields = [dot(turn_left, stacked(block)) for block in blocks]
    field = fields[0] if len(fields) == 1 else jnp.concatenate(fields, axis=0)
    high, low = split(field)
    contract = (((1,), (1,)), ((), ()))
    coefs = lax.dot_general(pick, high, contract, preferred_element_type=jnp.float32)
    coefs = coefs + lax.dot_general(pick, low, contract, preferred_element_type=jnp.float32)
    rows = pick.shape[0] // 4
    for at in range(4):
        coefs_ref[at] = coefs[at * rows : (at + 1) * rows]

    def body(at):
        orbs_ref[at] = product(get("synth", at), coefs_ref[at])

    each_part(small, body)
    for at, quadrant in enumerate(unfold([orbs_ref[at] for at in range(4)])):
        orbs_ref[at] = quadrant


def read_coefs(ref, lanes):
    block = jnp.concatenate([ref[at] for at in range(ref.shape[0])], axis=1)
    pad = lanes - block.shape[0]
    if pad:
        block = jnp.concatenate([block, jnp.zeros((pad, block.shape[1]), block.dtype)], axis=0)
    return block


def orbitals_kernel(count, shapes, where, pick_ref, *refs):
    get = table_getter(shapes, refs[count:-count - 2], where)
    out_refs, (all_ref, coefs_ref) = refs[-count - 2 : -2], refs[-2:]
    lanes = get("turn_right").shape[0] // 2
    blocks = [read_coefs(ref, lanes) for ref in refs[:count]]
    synthesize(True, blocks, pick_ref[...], get, coefs_ref, all_ref)
    for at in range(4):
        for block, out_ref in enumerate(out_refs):
            out_ref[at] = all_ref[at, :, block * lanes : (block + 1) * lanes]


def exchange_kernel(members, points, owners, sizes, begins, ends, ready, shapes, where, *refs):
    refs = list(refs)
    take = lambda count: [refs.pop(0) for _ in range(count)]
    prior_ref = None
    if begins:
        indices_refs = take(owners)
    else:
        pick_ref, own_ref, prior_ref = take(3)
    coef_refs = take(sum(sizes))
    get = table_getter(shapes, take(len(shapes) if where is None else 1), where)
    if ends:
        (out_ref,) = take(1)
    elif begins:
        pick_ref, own_ref, field_ref = take(3)
    else:
        (field_ref,) = take(1)
    visit_all_ref, work_all_ref, coefs_all_ref = take(3)
    if begins and ends:
        pick_ref, own_ref, field_ref = take(3)
    if begins:
        pick_ref[...] = pick_matrix(jnp.concatenate([ref[...] for ref in indices_refs], axis=1), get("codes").astype(jnp.float32), points)
    pick, turn_right = pick_ref[...], get("turn_right")
    lanes = turn_right.shape[0] // 2
    small = where is not None
    weight = get("weights").astype(jnp.float32)
    weight = weight[:, :lanes] + weight[:, lanes:]
    start = 0
    for step, size in enumerate(sizes):
        refs = [ref.at[:, :, : size * lanes] for ref in (visit_all_ref, work_all_ref, coefs_all_ref)]
        visit_ref, work_ref, coefs_ref = refs
        group_refs = coef_refs[start : start + size]
        start += size
        if ready:
            visit = [jnp.concatenate([ref[at] for ref in group_refs], axis=1) for at in range(4)]
        else:
            blocks = [read_coefs(ref, lanes) for ref in group_refs]
            synthesize(small, blocks, pick, get, coefs_ref, visit_ref)
            visit = [visit_ref[at] for at in range(4)]
        if begins and step == 0:
            for at in range(4):
                own_ref[at] = visit_ref[at, :, :lanes]
        weights = jnp.concatenate([weight] * size, axis=1)
        density = []
        for at in range(4):
            density.append(jnp.concatenate([own_ref[at]] * size, axis=1) * visit[at])
        density = unfold(density)
        if small:
            stages = (
                lambda at, part: product(get("forward", at), part[: get("forward", at).shape[1] // 3]),
                lambda at, part: turn(part, turn_right) * weights[: part.shape[0]],
                lambda at, part: turn(part, turn_right),
                lambda at, part: product(get("inverse", at), part),
            )
            potential = density
            for stage in stages:
                potential = [stage(at, part) for at, part in enumerate(potential)]
        else:
            for at, part in enumerate(density):
                work_ref[at] = part

            @pl.loop(0, 4)
            def poisson(at):
                spectrum = turn(product(get("forward", at), work_ref[at]), turn_right)
                spectrum = turn(spectrum * weights, turn_right)
                work_ref[at] = product(get("inverse", at), spectrum)

            potential = [work_ref[at] for at in range(4)]
        field = []
        for at, quadrant in enumerate(unfold(potential)):
            term = quadrant * visit[at]
            total = term[:, :lanes]
            for block in range(1, size):
                total = total + term[:, block * lanes : (block + 1) * lanes]
            if prior_ref is not None:
                total = total + prior_ref[at]
            if ends and step == len(sizes) - 1:
                field.append(total)
            else:
                field_ref[at] = total
        if not (ends and step == len(sizes) - 1):
            prior_ref = field_ref
    if ends:
        field = unfold(field)
        coefs = [product(get("project", at), field[at]) for at in range(4)]
        coefs = turn(jnp.concatenate(coefs, axis=0), turn_right)
        high, low = split(coefs.T)
        own_pick = pick[:, : out_ref.shape[1]]
        result = dot(high, own_pick) + dot(low, own_pick)
        out_ref[...] = result[: members * points]


def hold_kernel(*refs):
    semaphores = refs[-1]
    count = (len(refs) - 1) // 2
    copies = [
        pltpu.make_async_copy(refs[at], refs[count + at], semaphores.at[at]) for at in range(count)
    ]
    for copy in copies:
        copy.start()
    for copy in copies:
        copy.wait()


def hold(*values, flops=0):
    return pl.pallas_call(
        hold_kernel,
        out_shape=[jax.ShapeDtypeStruct(value.shape, value.dtype) for value in values],
        in_specs=[pl.BlockSpec(memory_space=pl.ANY)] * len(values),
        out_specs=[pl.BlockSpec(memory_space=pltpu.VMEM)] * len(values),
        scratch_shapes=[pltpu.SemaphoreType.DMA((len(values),))],
        cost_estimate=pl.CostEstimate(flops=flops, bytes_accessed=2**16, transcendentals=0),
        compiler_params=pltpu.CompilerParams(vmem_limit_bytes=16 * 2**20),
    )(*values)


def swap(value, axis, partner):
    count = lax.axis_size(axis)
    return lax.ppermute(value, axis, [(at, partner(at) % count) for at in range(count)])


def rest_of_ring(value, axis):
    count = lax.axis_size(axis)
    return [
        lax.ppermute(value, axis, [(at, (at + step) % count) for at in range(count)])
        for step in range(1, count)
    ]


def shards(stick_coefs, miller, stick_count):
    groups, members, points, per_owner = stick_coefs.shape
    owners = lax.axis_size("pw")
    batch = max(n for n in range(1, members + 1) if members % n == 0 and (n == 1 or n * points <= LANES))
    tables, small = build_tables(points, per_owner * owners, batch)
    shapes = {name: table.shape for name, table in tables.items()}
    where, held = None, list(tables.values())
    if small:
        packed, where = pack_tables(tables)
        held = [packed]
    values = [jnp.asarray(table) for table in held]
    own = stick_coefs.reshape(members * points, per_owner)
    others = rest_of_ring(own, "pw")
    position = jnp.arange(per_owner, dtype=jnp.int32)[None]
    indices = jnp.where(position < stick_count[0], miller, -1).astype(jnp.float32)
    indices = jnp.concatenate([indices, jnp.zeros((6, per_owner), jnp.float32)], axis=0)
    other_indices = rest_of_ring(indices, "pw")
    (own,) = hold(own)
    (indices,) = hold(indices, flops=5 * 10**9)
    indices = [indices] + other_indices

    ring = lax.axis_size("band")
    coefs = jnp.stack([own] + others)
    mate = swap(coefs, "band", lambda at: at ^ 1)
    got = swap(jnp.stack([coefs, mate]), "band", lambda at: at + 1 if at & 1 else at - 1 + ring)

    lanes = tables["turn_right"].shape[0] // 2
    n_place, n_picked = shapes["synth0" if small else "synth"][-2], shapes["codes"][0]
    vmem = pl.BlockSpec(memory_space=pltpu.VMEM)
    grid_shape = jax.ShapeDtypeStruct((4, n_place, lanes), jnp.float32)

    pick_shape = jax.ShapeDtypeStruct((4 * n_picked, per_owner * owners), jnp.bfloat16)
    out_shape = jax.ShapeDtypeStruct((batch * points, per_owner), jnp.float32)

    def call(sizes, carried, groups_in, out_shape, begins=False, ends=False, ready=False):
        wide = max(sizes) * lanes
        scratch = [
            pltpu.VMEM((4, n_place, wide), jnp.float32),
            pltpu.VMEM((4, 8 if small else n_place, wide), jnp.float32),
            pltpu.VMEM((4, n_picked, wide), jnp.float32),
        ]
        if begins and ends:
            scratch += [pltpu.VMEM(each.shape, each.dtype) for each in (pick_shape, grid_shape, grid_shape)]
        return pl.pallas_call(
            functools.partial(
                exchange_kernel, batch, points, owners, sizes, begins, ends, ready, shapes, where
            ),
            out_shape=out_shape,
            in_specs=[vmem] * (len(carried) + len(groups_in) + len(values)),
            out_specs=jax.tree.map(lambda _: vmem, out_shape),
            scratch_shapes=scratch,
            cost_estimate=pl.CostEstimate(flops=5 * 10**9, bytes_accessed=4 * 2**20, transcendentals=0),
            compiler_params=pltpu.CompilerParams(vmem_limit_bytes=(24 if small else 50) * 2**20),
        )(*carried, *groups_in, *values)

    def orbitals_of(pick, groups_in):
        count = len(groups_in)
        return pl.pallas_call(
            functools.partial(orbitals_kernel, count, shapes, where),
            out_shape=[grid_shape] * count,
            in_specs=[vmem] * (1 + count + len(values)),
            out_specs=[vmem] * count,
            scratch_shapes=[
                pltpu.VMEM((4, n_place, count * lanes), jnp.float32),
                pltpu.VMEM((4, n_picked, count * lanes), jnp.float32),
            ],
            cost_estimate=pl.CostEstimate(flops=10**9, bytes_accessed=2**20, transcendentals=0),
            compiler_params=pltpu.CompilerParams(vmem_limit_bytes=24 * 2**20),
        )(pick, *groups_in, *values)

    if small and batch == members:
        pick, orbs, field = call(
            (2,), indices, (coefs, mate), (pick_shape, grid_shape, grid_shape), begins=True
        )
        near, far = orbitals_of(pick, (got[0], got[1]))
        last = swap(near, "band", lambda at: at ^ 1)
        field = call((2,), (pick, orbs, field), (near, far), grid_shape, ready=True)
        result = call((1,), (pick, orbs, field), (last,), out_shape, ends=True, ready=True)
    else:
        last = swap(got[0], "band", lambda at: at ^ 1)

        def exchange(pieces):
            return call((2, 2, 1), indices, pieces, out_shape, begins=True, ends=True)

        def cut(piece):
            return piece.reshape(owners, -1, batch * points, per_owner).swapaxes(0, 1)

        pieces = (coefs, mate, got[0], got[1], last)
        if batch == members:
            result = exchange(pieces)
        else:
            result = lax.map(exchange, tuple(cut(piece) for piece in pieces))
    return result.reshape(groups, members, points, per_owner)


def solution(mesh):
    return jax.shard_map(
        shards,
        mesh=mesh,
        in_specs=(P("band", None, None, "pw"), P(None, "pw"), P("pw")),
        out_specs=P("band", None, None, "pw"),
        check_vma=False,
    )
```

```python
import functools
import math

import jax
import jax.numpy as jnp
import ml_dtypes
import numpy as np
from jax import lax
from jax.experimental import pallas as pl
from jax.experimental.pallas import tpu as pltpu
from jax.sharding import PartitionSpec as P

HALF = 2
kernel_scale = 4.0
screen_width = 16.0
LANES = 128
ROWS = 16
SMALL = 512
PARITIES = ("cc", "sc", "cs", "ss")


def round_up(value, unit):
    return -(-value // unit) * unit


def split_table(table):
    head = table.astype(np.float32).astype(ml_dtypes.bfloat16)
    rest = (table - head.astype(np.float64)).astype(np.float32).astype(ml_dtypes.bfloat16)
    return head, rest


@functools.lru_cache(maxsize=None)
def build_tables(points, sticks, members):
    signed = np.arange(points)
    signed = np.where(signed < points // 2, signed, signed - points)
    radius = signed[:, None] ** 2 + signed[None, :] ** 2
    limit = np.sort(radius.reshape(-1))[min(sticks, points * points) - 1]
    picked = sorted({(abs(b), abs(c)) for b in signed for c in signed if b * b + c * c <= limit})
    largest = max(b for b, _ in picked)
    grid = 4 * largest + 1 if 4 * largest + 1 < points else points

    def fold(value):
        value = value % points
        return min(value, points - value)

    pairs = set()
    for b1, c1 in picked:
        for b2, c2 in picked:
            for b in {fold(b1 + b2), fold(b1 - b2)}:
                for c in {fold(c1 + c2), fold(c1 - c2)}:
                    pairs.add((b, c))
    near = grid // 2 + 1

    def mirrored(value):
        return 2 * value % grid != 0

    def order(spots):
        return sorted(spots, key=lambda spot: (not mirrored(spot[0]), not mirrored(spot[1]), spot))

    pairs = order(pairs)
    place = order((y, z) for y in range(near) for z in range(near))
    place_weight = np.array([np.prod([1.0 if mirrored(v) else 0.5 for v in spot]) for spot in place])
    small = len(place) <= SMALL

    def wave(kind, freq, spot):
        angle = 2.0 * np.pi * ((freq[:, None] * spot[None, :]) % grid) / grid
        return np.cos(angle) if kind == "c" else np.sin(angle)

    def class_waves(kinds, freqs):
        freqs, spots = np.array(freqs), np.array(place)
        first = wave(kinds[0], freqs[:, 0], spots[:, 0])
        return first * wave(kinds[1], freqs[:, 1], spots[:, 1])

    def class_pairs(kinds):
        if not small:
            return pairs
        if kinds == "cs":
            return [(c, b) for b, c in class_pairs("sc")]
        return [p for p in pairs if all(kind == "c" or mirrored(v) for kind, v in zip(kinds, p))]

    def split_columns(table, rows, cols):
        full = np.zeros((rows, cols))
        full[: table.shape[0], : table.shape[1]] = table
        high, low = split_table(full)
        return np.concatenate([high, low, high], axis=1)

    n_place = round_up(len(place), ROWS)
    n_pairs = round_up(len(pairs), ROWS)
    n_picked = round_up(len(picked), ROWS)
    scale = points**-1.5
    by_parity = dict(synth=[], project=[], forward=[], inverse=[])
    for kinds in PARITIES:
        few = class_waves(kinds, picked)
        many = class_waves(kinds, class_pairs(kinds))
        rows, depth = n_pairs, n_place
        if small:
            rows = round_up(many.shape[0], ROWS)
            depth = round_up(1 + np.flatnonzero(np.abs(many).max(axis=0) > 1e-9)[-1], ROWS)
        few_back = -few * place_weight * scale * (points / grid) ** 2
        by_parity["synth"].append(split_columns(few.T * scale, n_place, n_picked))
        by_parity["project"].append(split_columns(few_back, n_picked, n_place))
        by_parity["forward"].append(split_columns((many * place_weight)[:, :depth], rows, depth))
        by_parity["inverse"].append(split_columns(many.T, n_place, rows))

    index = np.arange(points)
    angle = 2.0 * np.pi * ((index[:, None] * index[None, :]) % points) / points
    cas = np.cos(angle) + np.sin(angle)
    lanes = round_up(members * points, LANES)
    block = np.zeros((lanes, lanes))
    for member in range(members):
        at = member * points
        block[at : at + points, at : at + points] = cas
    high, low = split_table(block)
    turn_left = np.concatenate([high, low, high], axis=1)
    turn_right = np.block([[high, low], [high, low]])

    squares = signed.astype(np.float64) ** 2
    freqs = np.array(pairs)
    total = (freqs[:, 0] ** 2 + freqs[:, 1] ** 2)[:, None] + squares[None, :]
    scaled = total / screen_width
    safe = np.where(total > 0, scaled, 1.0)
    kernel = kernel_scale * np.where(total > 0, -np.expm1(-safe) / safe, 1.0)
    double = np.where(mirrored(freqs), 2.0, 1.0)
    kernel = kernel * (double[:, 0] * double[:, 1])[:, None]
    kernel = kernel * (points / grid) ** 2 / float(points**3)
    weights = np.zeros((n_pairs, lanes))
    for member in range(members):
        weights[: len(pairs), member * points : (member + 1) * points] = kernel

    codes = np.full((n_picked, LANES), -7.0)
    for at, (b, c) in enumerate(picked):
        codes[at, 0], codes[at, 1] = b, c
    tables = dict(
        turn_left=turn_left,
        turn_right=turn_right,
        weights=np.concatenate(split_table(weights), axis=1),
        codes=codes.astype(ml_dtypes.bfloat16),
    )
    for name, each in by_parity.items():
        if small:
            tables.update({name + str(at): table for at, table in enumerate(each)})
        else:
            tables[name] = np.stack(each)
    return tables, small


def pack_tables(tables):
    parities = [str(at) for at in range(len(PARITIES))]
    shelves = [("forward" + at,) for at in parities] + [("project" + at,) for at in parities]
    shelves += [("inverse" + at, "synth" + at) for at in parities]
    shelves.append(("turn_left", "turn_right", "weights", "codes"))
    where, row, width = {}, 0, 0
    for shelf in shelves:
        column = 0
        for name in shelf:
            where[name] = (row, column)
            column += round_up(tables[name].shape[1], LANES)
        row += round_up(max(tables[name].shape[0] for name in shelf), ROWS)
        width = max(width, column)
    packed = np.zeros((row, width), ml_dtypes.bfloat16)
    for name, (first, column) in where.items():
        rows, cols = tables[name].shape
        packed[first : first + rows, column : column + cols] = tables[name]
    return packed, where


def table_getter(shapes, refs, where):
    def get(name, at=None):
        if where is None:
            ref = refs[list(shapes).index(name)]
            return ref[...] if at is None else ref[at]
        name = name if at is None else name + str(at)
        (first, column), (rows, cols) = where[name], shapes[name]
        return refs[0][first : first + rows, column : column + cols]

    return get


def dot(left, right):
    return jnp.dot(left, right, preferred_element_type=jnp.float32)


def split(value):
    high = value.astype(jnp.bfloat16)
    low = (value - high.astype(jnp.float32)).astype(jnp.bfloat16)
    return high, low


def stacked(value):
    high, low = split(value)
    return jnp.concatenate([high, high, low], axis=0)


def product(table, value):
    depth, lanes = value.shape
    if lanes > LANES or depth <= LANES:
        return dot(table, stacked(value))
    halves = jnp.concatenate(split(value), axis=1)
    out = dot(table[:, : 2 * depth], jnp.concatenate([halves, halves], axis=0))
    return out[:, :lanes] + out[:, lanes:]


def pick_matrix(indices, codes, points):
    first, second = indices[0:1], indices[1:2]
    alive = first >= 0.0
    signed_first = jnp.where(first < points // 2, first, first - points)
    signed_second = jnp.where(second < points // 2, second, second - points)
    first_same = codes[:, 0:1] == jnp.where(alive, jnp.abs(signed_first), -1.0)
    one = jnp.where(first_same & (codes[:, 1:2] == jnp.abs(signed_second)), 1.0, 0.0)
    sign_first = jnp.where(signed_first < 0.0, -1.0, 1.0)
    sign_second = jnp.where(signed_second < 0.0, -1.0, 1.0)
    parts = [one, one * sign_first, one * sign_second, one * (sign_first * sign_second)]
    return jnp.concatenate(parts, axis=0).astype(jnp.bfloat16)


def unfold(parts):
    even, odd = parts[0] + parts[2], parts[1] + parts[3]
    even_less, odd_less = parts[0] - parts[2], parts[1] - parts[3]
    return [even + odd, even - odd, even_less + odd_less, even_less - odd_less]


def turn(value, turn_right):
    lanes = turn_right.shape[0] // 2
    outs = []
    for at in range(0, value.shape[1], lanes):
        high, low = split(value[:, at : at + lanes])
        out = dot(jnp.concatenate([high, low], axis=1), turn_right)
        outs.append(out[:, :lanes] + out[:, lanes:])
    return outs[0] if len(outs) == 1 else jnp.concatenate(outs, axis=1)


def each_part(small, body):
    if small:
        for at in range(4):
            body(at)
    else:
        pl.loop(0, 4)(body)


def synthesize(small, blocks, pick, get, coefs_ref, orbs_ref):
    turn_left = get("turn_left")
    fields = [dot(turn_left, stacked(block)) for block in blocks]
    field = fields[0] if len(fields) == 1 else jnp.concatenate(fields, axis=0)
    high, low = split(field)
    contract = (((1,), (1,)), ((), ()))
    coefs = lax.dot_general(pick, high, contract, preferred_element_type=jnp.float32)
    coefs = coefs + lax.dot_general(pick, low, contract, preferred_element_type=jnp.float32)
    rows = pick.shape[0] // 4
    for at in range(4):
        coefs_ref[at] = coefs[at * rows : (at + 1) * rows]

    def body(at):
        orbs_ref[at] = product(get("synth", at), coefs_ref[at])

    each_part(small, body)
    for at, quadrant in enumerate(unfold([orbs_ref[at] for at in range(4)])):
        orbs_ref[at] = quadrant


def read_coefs(ref, lanes):
    block = jnp.concatenate([ref[at] for at in range(ref.shape[0])], axis=1)
    pad = lanes - block.shape[0]
    if pad:
        block = jnp.concatenate([block, jnp.zeros((pad, block.shape[1]), block.dtype)], axis=0)
    return block


def orbitals_kernel(count, shapes, where, pick_ref, *refs):
    get = table_getter(shapes, refs[count:-count - 2], where)
    out_refs, (all_ref, coefs_ref) = refs[-count - 2 : -2], refs[-2:]
    lanes = get("turn_right").shape[0] // 2
    blocks = [read_coefs(ref, lanes) for ref in refs[:count]]
    synthesize(True, blocks, pick_ref[...], get, coefs_ref, all_ref)
    for at in range(4):
        for block, out_ref in enumerate(out_refs):
            out_ref[at] = all_ref[at, :, block * lanes : (block + 1) * lanes]


def exchange_kernel(members, points, owners, sizes, begins, ends, ready, shapes, where, *refs):
    refs = list(refs)
    take = lambda count: [refs.pop(0) for _ in range(count)]
    prior_ref = None
    if begins:
        indices_refs = take(owners)
    else:
        pick_ref, own_ref, prior_ref = take(3)
    coef_refs = take(sum(sizes))
    get = table_getter(shapes, take(len(shapes) if where is None else 1), where)
    if ends:
        (out_ref,) = take(1)
    elif begins:
        pick_ref, own_ref, field_ref = take(3)
    else:
        (field_ref,) = take(1)
    visit_all_ref, work_all_ref, coefs_all_ref = take(3)
    if begins and ends:
        pick_ref, own_ref, field_ref = take(3)
    if begins:
        pick_ref[...] = pick_matrix(jnp.concatenate([ref[...] for ref in indices_refs], axis=1), get("codes").astype(jnp.float32), points)
    pick, turn_right = pick_ref[...], get("turn_right")
    lanes = turn_right.shape[0] // 2
    small = where is not None
    weight = get("weights").astype(jnp.float32)
    weight = weight[:, :lanes] + weight[:, lanes:]
    start = 0
    for step, size in enumerate(sizes):
        refs = [ref.at[:, :, : size * lanes] for ref in (visit_all_ref, work_all_ref, coefs_all_ref)]
        visit_ref, work_ref, coefs_ref = refs
        group_refs = coef_refs[start : start + size]
        start += size
        if ready:
            visit = [jnp.concatenate([ref[at] for ref in group_refs], axis=1) for at in range(4)]
        else:
            blocks = [read_coefs(ref, lanes) for ref in group_refs]
            synthesize(small, blocks, pick, get, coefs_ref, visit_ref)
            visit = [visit_ref[at] for at in range(4)]
        if begins and step == 0:
            for at in range(4):
                own_ref[at] = visit_ref[at, :, :lanes]
        weights = jnp.concatenate([weight] * size, axis=1)
        density = []
        for at in range(4):
            density.append(jnp.concatenate([own_ref[at]] * size, axis=1) * visit[at])
        density = unfold(density)
        if small:
            stages = (
                lambda at, part: product(get("forward", at), part[: get("forward", at).shape[1] // 3]),
                lambda at, part: turn(part, turn_right) * weights[: part.shape[0]],
                lambda at, part: turn(part, turn_right),
                lambda at, part: product(get("inverse", at), part),
            )
            potential = density
            for stage in stages:
                potential = [stage(at, part) for at, part in enumerate(potential)]
        else:
            for at, part in enumerate(density):
                work_ref[at] = part

            @pl.loop(0, 4)
            def poisson(at):
                spectrum = turn(product(get("forward", at), work_ref[at]), turn_right)
                spectrum = turn(spectrum * weights, turn_right)
                work_ref[at] = product(get("inverse", at), spectrum)

            potential = [work_ref[at] for at in range(4)]
        field = []
        for at, quadrant in enumerate(unfold(potential)):
            term = quadrant * visit[at]
            total = term[:, :lanes]
            for block in range(1, size):
                total = total + term[:, block * lanes : (block + 1) * lanes]
            if prior_ref is not None:
                total = total + prior_ref[at]
            if ends and step == len(sizes) - 1:
                field.append(total)
            else:
                field_ref[at] = total
        if not (ends and step == len(sizes) - 1):
            prior_ref = field_ref
    if ends:
        field = unfold(field)
        coefs = [product(get("project", at), field[at]) for at in range(4)]
        coefs = turn(jnp.concatenate(coefs, axis=0), turn_right)
        high, low = split(coefs.T)
        own_pick = pick[:, : out_ref.shape[1]]
        result = dot(high, own_pick) + dot(low, own_pick)
        out_ref[...] = result[: members * points]


def hold_kernel(*refs):
    semaphores = refs[-1]
    count = (len(refs) - 1) // 2
    copies = [
        pltpu.make_async_copy(refs[at], refs[count + at], semaphores.at[at]) for at in range(count)
    ]
    for copy in copies:
        copy.start()
    for copy in copies:
        copy.wait()


def hold(*values, flops=0):
    return pl.pallas_call(
        hold_kernel,
        out_shape=[jax.ShapeDtypeStruct(value.shape, value.dtype) for value in values],
        in_specs=[pl.BlockSpec(memory_space=pl.ANY)] * len(values),
        out_specs=[pl.BlockSpec(memory_space=pltpu.VMEM)] * len(values),
        scratch_shapes=[pltpu.SemaphoreType.DMA((len(values),))],
        cost_estimate=pl.CostEstimate(flops=flops, bytes_accessed=2**16, transcendentals=0),
        compiler_params=pltpu.CompilerParams(vmem_limit_bytes=16 * 2**20),
    )(*values)


def swap(value, axis, partner):
    count = lax.axis_size(axis)
    return lax.ppermute(value, axis, [(at, partner(at) % count) for at in range(count)])


def rest_of_ring(value, axis):
    count = lax.axis_size(axis)
    return [
        lax.ppermute(value, axis, [(at, (at + step) % count) for at in range(count)])
        for step in range(1, count)
    ]


def shards(stick_coefs, miller, stick_count):
    groups, members, points, per_owner = stick_coefs.shape
    owners = lax.axis_size("pw")
    batch = max(n for n in range(1, members + 1) if members % n == 0 and (n == 1 or n * points <= LANES))
    tables, small = build_tables(points, per_owner * owners, batch)
    shapes = {name: table.shape for name, table in tables.items()}
    where, held = None, list(tables.values())
    if small:
        packed, where = pack_tables(tables)
        held = [packed]
    values = [jnp.asarray(table) for table in held]
    own = stick_coefs.reshape(members * points, per_owner)
    others = rest_of_ring(own, "pw")
    position = jnp.arange(per_owner, dtype=jnp.int32)[None]
    indices = jnp.where(position < stick_count[0], miller, -1).astype(jnp.float32)
    indices = jnp.concatenate([indices, jnp.zeros((6, per_owner), jnp.float32)], axis=0)
    other_indices = rest_of_ring(indices, "pw")
    (own,) = hold(own)
    (indices,) = hold(indices, flops=5 * 10**9)
    indices = [indices] + other_indices

    ring = lax.axis_size("band")
    coefs = jnp.stack([own] + others)
    mate = swap(coefs, "band", lambda at: at ^ 1)
    got = swap(jnp.stack([coefs, mate]), "band", lambda at: at + 1 if at & 1 else at - 1 + ring)

    lanes = tables["turn_right"].shape[0] // 2
    n_place, n_picked = shapes["synth0" if small else "synth"][-2], shapes["codes"][0]
    vmem = pl.BlockSpec(memory_space=pltpu.VMEM)
    grid_shape = jax.ShapeDtypeStruct((4, n_place, lanes), jnp.float32)

    pick_shape = jax.ShapeDtypeStruct((4 * n_picked, per_owner * owners), jnp.bfloat16)
    out_shape = jax.ShapeDtypeStruct((batch * points, per_owner), jnp.float32)

    def call(sizes, carried, groups_in, out_shape, begins=False, ends=False, ready=False):
        wide = max(sizes) * lanes
        scratch = [
            pltpu.VMEM((4, n_place, wide), jnp.float32),
            pltpu.VMEM((4, 8 if small else n_place, wide), jnp.float32),
            pltpu.VMEM((4, n_picked, wide), jnp.float32),
        ]
        if begins and ends:
            scratch += [pltpu.VMEM(each.shape, each.dtype) for each in (pick_shape, grid_shape, grid_shape)]
        return pl.pallas_call(
            functools.partial(
                exchange_kernel, batch, points, owners, sizes, begins, ends, ready, shapes, where
            ),
            out_shape=out_shape,
            in_specs=[vmem] * (len(carried) + len(groups_in) + len(values)),
            out_specs=jax.tree.map(lambda _: vmem, out_shape),
            scratch_shapes=scratch,
            cost_estimate=pl.CostEstimate(flops=5 * 10**9, bytes_accessed=4 * 2**20, transcendentals=0),
            compiler_params=pltpu.CompilerParams(vmem_limit_bytes=(24 if small else 50) * 2**20),
        )(*carried, *groups_in, *values)

    def orbitals_of(pick, groups_in):
        count = len(groups_in)
        return pl.pallas_call(
            functools.partial(orbitals_kernel, count, shapes, where),
            out_shape=[grid_shape] * count,
            in_specs=[vmem] * (1 + count + len(values)),
            out_specs=[vmem] * count,
            scratch_shapes=[
                pltpu.VMEM((4, n_place, count * lanes), jnp.float32),
                pltpu.VMEM((4, n_picked, count * lanes), jnp.float32),
            ],
            cost_estimate=pl.CostEstimate(flops=10**9, bytes_accessed=2**20, transcendentals=0),
            compiler_params=pltpu.CompilerParams(vmem_limit_bytes=24 * 2**20),
        )(pick, *groups_in, *values)

    if small and batch == members:
        pick, orbs, field = call(
            (2,), indices, (coefs, mate), (pick_shape, grid_shape, grid_shape), begins=True
        )
        near, far = orbitals_of(pick, (got[0], got[1]))
        last = swap(near, "band", lambda at: at ^ 1)
        field = call((2,), (pick, orbs, field), (near, far), grid_shape, ready=True)
        result = call((1,), (pick, orbs, field), (last,), out_shape, ends=True, ready=True)
    else:
        last = swap(got[0], "band", lambda at: at ^ 1)

        def exchange(pieces):
            return call((2, 2, 1), indices, pieces, out_shape, begins=True, ends=True)

        def cut(piece):
            return piece.reshape(owners, -1, batch * points, per_owner).swapaxes(0, 1)

        pieces = (coefs, mate, got[0], got[1], last)
        if batch == members:
            result = exchange(pieces)
        else:
            result = lax.map(exchange, tuple(cut(piece) for piece in pieces))
    return result.reshape(groups, members, points, per_owner)


def solution(mesh):
    return jax.shard_map(
        shards,
        mesh=mesh,
        in_specs=(P("band", None, None, "pw"), P(None, "pw"), P("pw")),
        out_specs=P("band", None, None, "pw"),
        check_vma=False,
    )
```

```python
import functools
import math

import jax
import jax.numpy as jnp
import ml_dtypes
import numpy as np
from jax import lax
from jax.experimental import pallas as pl
from jax.experimental.pallas import tpu as pltpu
from jax.sharding import PartitionSpec as P

HALF = 2
kernel_scale = 4.0
screen_width = 16.0
LANES = 128
ROWS = 16
SMALL = 512
PARITIES = ("cc", "sc", "cs", "ss")


def round_up(value, unit):
    return -(-value // unit) * unit


def split_table(table):
    head = table.astype(np.float32).astype(ml_dtypes.bfloat16)
    rest = (table - head.astype(np.float64)).astype(np.float32).astype(ml_dtypes.bfloat16)
    return head, rest


@functools.lru_cache(maxsize=None)
def build_tables(points, sticks, members):
    signed = np.arange(points)
    signed = np.where(signed < points // 2, signed, signed - points)
    radius = signed[:, None] ** 2 + signed[None, :] ** 2
    limit = np.sort(radius.reshape(-1))[min(sticks, points * points) - 1]
    picked = sorted({(abs(b), abs(c)) for b in signed for c in signed if b * b + c * c <= limit})
    largest = max(b for b, _ in picked)
    grid = 4 * largest + 1 if 4 * largest + 1 < points else points

    def fold(value):
        value = value % points
        return min(value, points - value)

    pairs = set()
    for b1, c1 in picked:
        for b2, c2 in picked:
            for b in {fold(b1 + b2), fold(b1 - b2)}:
                for c in {fold(c1 + c2), fold(c1 - c2)}:
                    pairs.add((b, c))
    near = grid // 2 + 1

    def mirrored(value):
        return 2 * value % grid != 0

    def order(spots):
        return sorted(spots, key=lambda spot: (not mirrored(spot[0]), not mirrored(spot[1]), spot))

    pairs = order(pairs)
    place = order((y, z) for y in range(near) for z in range(near))
    place_weight = np.array([np.prod([1.0 if mirrored(v) else 0.5 for v in spot]) for spot in place])
    small = len(place) <= SMALL

    def wave(kind, freq, spot):
        angle = 2.0 * np.pi * ((freq[:, None] * spot[None, :]) % grid) / grid
        return np.cos(angle) if kind == "c" else np.sin(angle)

    def class_waves(kinds, freqs):
        freqs, spots = np.array(freqs), np.array(place)
        first = wave(kinds[0], freqs[:, 0], spots[:, 0])
        return first * wave(kinds[1], freqs[:, 1], spots[:, 1])

    def class_pairs(kinds):
        if not small:
            return pairs
        if kinds == "cs":
            return [(c, b) for b, c in class_pairs("sc")]
        return [p for p in pairs if all(kind == "c" or mirrored(v) for kind, v in zip(kinds, p))]

    def split_columns(table, rows, cols):
        full = np.zeros((rows, cols))
        full[: table.shape[0], : table.shape[1]] = table
        high, low = split_table(full)
        return np.concatenate([high, low, high], axis=1)

    n_place = round_up(len(place), ROWS)
    n_pairs = round_up(len(pairs), ROWS)
    n_picked = round_up(len(picked), ROWS)
    scale = points**-1.5
    by_parity = dict(synth=[], project=[], forward=[], inverse=[])
    for kinds in PARITIES:
        few = class_waves(kinds, picked)
        many = class_waves(kinds, class_pairs(kinds))
        rows, depth = n_pairs, n_place
        if small:
            rows = round_up(many.shape[0], ROWS)
            depth = round_up(1 + np.flatnonzero(np.abs(many).max(axis=0) > 1e-9)[-1], ROWS)
        few_back = -few * place_weight * scale * (points / grid) ** 2
        by_parity["synth"].append(split_columns(few.T * scale, n_place, n_picked))
        by_parity["project"].append(split_columns(few_back, n_picked, n_place))
        by_parity["forward"].append(split_columns((many * place_weight)[:, :depth], rows, depth))
        by_parity["inverse"].append(split_columns(many.T, n_place, rows))

    index = np.arange(points)
    angle = 2.0 * np.pi * ((index[:, None] * index[None, :]) % points) / points
    cas = np.cos(angle) + np.sin(angle)
    lanes = round_up(members * points, LANES)
    block = np.zeros((lanes, lanes))
    for member in range(members):
        at = member * points
        block[at : at + points, at : at + points] = cas
    high, low = split_table(block)
    turn_left = np.concatenate([high, low, high], axis=1)
    turn_right = np.block([[high, low], [high, low]])

    squares = signed.astype(np.float64) ** 2
    freqs = np.array(pairs)
    total = (freqs[:, 0] ** 2 + freqs[:, 1] ** 2)[:, None] + squares[None, :]
    scaled = total / screen_width
    safe = np.where(total > 0, scaled, 1.0)
    kernel = kernel_scale * np.where(total > 0, -np.expm1(-safe) / safe, 1.0)
    double = np.where(mirrored(freqs), 2.0, 1.0)
    kernel = kernel * (double[:, 0] * double[:, 1])[:, None]
    kernel = kernel * (points / grid) ** 2 / float(points**3)
    weights = np.zeros((n_pairs, lanes))
    for member in range(members):
        weights[: len(pairs), member * points : (member + 1) * points] = kernel

    codes = np.full((n_picked, LANES), -7.0)
    for at, (b, c) in enumerate(picked):
        codes[at, 0], codes[at, 1] = b, c
    tables = dict(
        turn_left=turn_left,
        turn_right=turn_right,
        weights=np.concatenate(split_table(weights), axis=1),
        codes=codes.astype(ml_dtypes.bfloat16),
    )
    for name, each in by_parity.items():
        if small:
            tables.update({name + str(at): table for at, table in enumerate(each)})
        else:
            tables[name] = np.stack(each)
    return tables, small


def pack_tables(tables):
    parities = [str(at) for at in range(len(PARITIES))]
    shelves = [("forward" + at,) for at in parities] + [("project" + at,) for at in parities]
    shelves += [("inverse" + at, "synth" + at) for at in parities]
    shelves.append(("turn_left", "turn_right", "weights", "codes"))
    where, row, width = {}, 0, 0
    for shelf in shelves:
        column = 0
        for name in shelf:
            where[name] = (row, column)
            column += round_up(tables[name].shape[1], LANES)
        row += round_up(max(tables[name].shape[0] for name in shelf), ROWS)
        width = max(width, column)
    packed = np.zeros((row, width), ml_dtypes.bfloat16)
    for name, (first, column) in where.items():
        rows, cols = tables[name].shape
        packed[first : first + rows, column : column + cols] = tables[name]
    return packed, where


def table_getter(shapes, refs, where):
    def get(name, at=None):
        if where is None:
            ref = refs[list(shapes).index(name)]
            return ref[...] if at is None else ref[at]
        name = name if at is None else name + str(at)
        (first, column), (rows, cols) = where[name], shapes[name]
        return refs[0][first : first + rows, column : column + cols]

    return get


def dot(left, right):
    return jnp.dot(left, right, preferred_element_type=jnp.float32)


def split(value):
    high = value.astype(jnp.bfloat16)
    low = (value - high.astype(jnp.float32)).astype(jnp.bfloat16)
    return high, low


def stacked(value):
    high, low = split(value)
    return jnp.concatenate([high, high, low], axis=0)


def product(table, value):
    depth, lanes = value.shape
    if lanes > LANES or depth <= LANES:
        return dot(table, stacked(value))
    halves = jnp.concatenate(split(value), axis=1)
    out = dot(table[:, : 2 * depth], jnp.concatenate([halves, halves], axis=0))
    return out[:, :lanes] + out[:, lanes:]


def pick_matrix(indices, codes, points):
    first, second = indices[0:1], indices[1:2]
    alive = first >= 0.0
    signed_first = jnp.where(first < points // 2, first, first - points)
    signed_second = jnp.where(second < points // 2, second, second - points)
    first_same = codes[:, 0:1] == jnp.where(alive, jnp.abs(signed_first), -1.0)
    one = jnp.where(first_same & (codes[:, 1:2] == jnp.abs(signed_second)), 1.0, 0.0)
    sign_first = jnp.where(signed_first < 0.0, -1.0, 1.0)
    sign_second = jnp.where(signed_second < 0.0, -1.0, 1.0)
    parts = [one, one * sign_first, one * sign_second, one * (sign_first * sign_second)]
    return jnp.concatenate(parts, axis=0).astype(jnp.bfloat16)


def unfold(parts):
    even, odd = parts[0] + parts[2], parts[1] + parts[3]
    even_less, odd_less = parts[0] - parts[2], parts[1] - parts[3]
    return [even + odd, even - odd, even_less + odd_less, even_less - odd_less]


def turn(value, turn_right):
    lanes = turn_right.shape[0] // 2
    outs = []
    for at in range(0, value.shape[1], lanes):
        high, low = split(value[:, at : at + lanes])
        out = dot(jnp.concatenate([high, low], axis=1), turn_right)
        outs.append(out[:, :lanes] + out[:, lanes:])
    return outs[0] if len(outs) == 1 else jnp.concatenate(outs, axis=1)


def each_part(small, body):
    if small:
        for at in range(4):
            body(at)
    else:
        pl.loop(0, 4)(body)


def synthesize(small, blocks, pick, get, coefs_ref, orbs_ref):
    turn_left = get("turn_left")
    fields = [dot(turn_left, stacked(block)) for block in blocks]
    field = fields[0] if len(fields) == 1 else jnp.concatenate(fields, axis=0)
    high, low = split(field)
    contract = (((1,), (1,)), ((), ()))
    coefs = lax.dot_general(pick, high, contract, preferred_element_type=jnp.float32)
    coefs = coefs + lax.dot_general(pick, low, contract, preferred_element_type=jnp.float32)
    rows = pick.shape[0] // 4
    for at in range(4):
        coefs_ref[at] = coefs[at * rows : (at + 1) * rows]

    def body(at):
        orbs_ref[at] = product(get("synth", at), coefs_ref[at])

    each_part(small, body)
    for at, quadrant in enumerate(unfold([orbs_ref[at] for at in range(4)])):
        orbs_ref[at] = quadrant


def read_coefs(ref, lanes):
    block = jnp.concatenate([ref[at] for at in range(ref.shape[0])], axis=1)
    pad = lanes - block.shape[0]
    if pad:
        block = jnp.concatenate([block, jnp.zeros((pad, block.shape[1]), block.dtype)], axis=0)
    return block


def orbitals_kernel(count, shapes, where, pick_ref, *refs):
    get = table_getter(shapes, refs[count:-count - 2], where)
    out_refs, (all_ref, coefs_ref) = refs[-count - 2 : -2], refs[-2:]
    lanes = get("turn_right").shape[0] // 2
    blocks = [read_coefs(ref, lanes) for ref in refs[:count]]
    synthesize(True, blocks, pick_ref[...], get, coefs_ref, all_ref)
    for at in range(4):
        for block, out_ref in enumerate(out_refs):
            out_ref[at] = all_ref[at, :, block * lanes : (block + 1) * lanes]


def exchange_kernel(members, points, owners, sizes, begins, ends, ready, shapes, where, *refs):
    refs = list(refs)
    take = lambda count: [refs.pop(0) for _ in range(count)]
    prior_ref = None
    if begins:
        indices_refs = take(owners)
    else:
        pick_ref, own_ref, prior_ref = take(3)
    coef_refs = take(sum(sizes))
    get = table_getter(shapes, take(len(shapes) if where is None else 1), where)
    if ends:
        (out_ref,) = take(1)
    elif begins:
        pick_ref, own_ref, field_ref = take(3)
    else:
        (field_ref,) = take(1)
    visit_all_ref, work_all_ref, coefs_all_ref = take(3)
    if begins and ends:
        pick_ref, own_ref, field_ref = take(3)
    if begins:
        pick_ref[...] = pick_matrix(jnp.concatenate([ref[...] for ref in indices_refs], axis=1), get("codes").astype(jnp.float32), points)
    pick, turn_right = pick_ref[...], get("turn_right")
    lanes = turn_right.shape[0] // 2
    small = where is not None
    weight = get("weights").astype(jnp.float32)
    weight = weight[:, :lanes] + weight[:, lanes:]
    start = 0
    for step, size in enumerate(sizes):
        refs = [ref.at[:, :, : size * lanes] for ref in (visit_all_ref, work_all_ref, coefs_all_ref)]
        visit_ref, work_ref, coefs_ref = refs
        group_refs = coef_refs[start : start + size]
        start += size
        if ready:
            visit = [jnp.concatenate([ref[at] for ref in group_refs], axis=1) for at in range(4)]
        else:
            blocks = [read_coefs(ref, lanes) for ref in group_refs]
            synthesize(small, blocks, pick, get, coefs_ref, visit_ref)
            visit = [visit_ref[at] for at in range(4)]
        if begins and step == 0:
            for at in range(4):
                own_ref[at] = visit_ref[at, :, :lanes]
        weights = jnp.concatenate([weight] * size, axis=1)
        density = []
        for at in range(4):
            density.append(jnp.concatenate([own_ref[at]] * size, axis=1) * visit[at])
        density = unfold(density)
        if small:
            stages = (
                lambda at, part: product(get("forward", at), part[: get("forward", at).shape[1] // 3]),
                lambda at, part: turn(part, turn_right) * weights[: part.shape[0]],
                lambda at, part: turn(part, turn_right),
                lambda at, part: product(get("inverse", at), part),
            )
            potential = density
            for stage in stages:
                potential = [stage(at, part) for at, part in enumerate(potential)]
        else:
            for at, part in enumerate(density):
                work_ref[at] = part

            @pl.loop(0, 4)
            def poisson(at):
                spectrum = turn(product(get("forward", at), work_ref[at]), turn_right)
                spectrum = turn(spectrum * weights, turn_right)
                work_ref[at] = product(get("inverse", at), spectrum)

            potential = [work_ref[at] for at in range(4)]
        field = []
        for at, quadrant in enumerate(unfold(potential)):
            term = quadrant * visit[at]
            total = term[:, :lanes]
            for block in range(1, size):
                total = total + term[:, block * lanes : (block + 1) * lanes]
            if prior_ref is not None:
                total = total + prior_ref[at]
            if ends and step == len(sizes) - 1:
                field.append(total)
            else:
                field_ref[at] = total
        if not (ends and step == len(sizes) - 1):
            prior_ref = field_ref
    if ends:
        field = unfold(field)
        coefs = [product(get("project", at), field[at]) for at in range(4)]
        coefs = turn(jnp.concatenate(coefs, axis=0), turn_right)
        high, low = split(coefs.T)
        own_pick = pick[:, : out_ref.shape[1]]
        result = dot(high, own_pick) + dot(low, own_pick)
        out_ref[...] = result[: members * points]


def hold_kernel(*refs):
    semaphores = refs[-1]
    count = (len(refs) - 1) // 2
    copies = [
        pltpu.make_async_copy(refs[at], refs[count + at], semaphores.at[at]) for at in range(count)
    ]
    for copy in copies:
        copy.start()
    for copy in copies:
        copy.wait()


def hold(*values, flops=0):
    return pl.pallas_call(
        hold_kernel,
        out_shape=[jax.ShapeDtypeStruct(value.shape, value.dtype) for value in values],
        in_specs=[pl.BlockSpec(memory_space=pl.ANY)] * len(values),
        out_specs=[pl.BlockSpec(memory_space=pltpu.VMEM)] * len(values),
        scratch_shapes=[pltpu.SemaphoreType.DMA((len(values),))],
        cost_estimate=pl.CostEstimate(flops=flops, bytes_accessed=2**16, transcendentals=0),
        compiler_params=pltpu.CompilerParams(vmem_limit_bytes=16 * 2**20),
    )(*values)


def swap(value, axis, partner):
    count = lax.axis_size(axis)
    return lax.ppermute(value, axis, [(at, partner(at) % count) for at in range(count)])


def rest_of_ring(value, axis):
    count = lax.axis_size(axis)
    return [
        lax.ppermute(value, axis, [(at, (at + step) % count) for at in range(count)])
        for step in range(1, count)
    ]


def shards(stick_coefs, miller, stick_count):
    groups, members, points, per_owner = stick_coefs.shape
    owners = lax.axis_size("pw")
    batch = max(n for n in range(1, members + 1) if members % n == 0 and (n == 1 or n * points <= LANES))
    tables, small = build_tables(points, per_owner * owners, batch)
    shapes = {name: table.shape for name, table in tables.items()}
    where, held = None, list(tables.values())
    if small:
        packed, where = pack_tables(tables)
        held = [packed]
    values = [jnp.asarray(table) for table in held]
    own = stick_coefs.reshape(members * points, per_owner)
    others = rest_of_ring(own, "pw")
    early = swap(own, "band", lambda at: at ^ 1)
    position = jnp.arange(per_owner, dtype=jnp.int32)[None]
    indices = jnp.where(position < stick_count[0], miller, -1).astype(jnp.float32)
    indices = jnp.concatenate([indices, jnp.zeros((6, per_owner), jnp.float32)], axis=0)
    other_indices = rest_of_ring(indices, "pw")
    (own,) = hold(own)
    (indices,) = hold(indices, flops=5 * 10**9)
    indices = [indices] + other_indices

    ring = lax.axis_size("band")
    coefs = jnp.stack([own] + others)
    mate = jnp.stack([early] + [swap(other, "band", lambda at: at ^ 1) for other in others])
    got = swap(jnp.stack([coefs, mate]), "band", lambda at: at + 1 if at & 1 else at - 1 + ring)

    lanes = tables["turn_right"].shape[0] // 2
    n_place, n_picked = shapes["synth0" if small else "synth"][-2], shapes["codes"][0]
    vmem = pl.BlockSpec(memory_space=pltpu.VMEM)
    grid_shape = jax.ShapeDtypeStruct((4, n_place, lanes), jnp.float32)

    pick_shape = jax.ShapeDtypeStruct((4 * n_picked, per_owner * owners), jnp.bfloat16)
    out_shape = jax.ShapeDtypeStruct((batch * points, per_owner), jnp.float32)

    def call(sizes, carried, groups_in, out_shape, begins=False, ends=False, ready=False):
        wide = max(sizes) * lanes
        scratch = [
            pltpu.VMEM((4, n_place, wide), jnp.float32),
            pltpu.VMEM((4, 8 if small else n_place, wide), jnp.float32),
            pltpu.VMEM((4, n_picked, wide), jnp.float32),
        ]
        if begins and ends:
            scratch += [pltpu.VMEM(each.shape, each.dtype) for each in (pick_shape, grid_shape, grid_shape)]
        return pl.pallas_call(
            functools.partial(
                exchange_kernel, batch, points, owners, sizes, begins, ends, ready, shapes, where
            ),
            out_shape=out_shape,
            in_specs=[vmem] * (len(carried) + len(groups_in) + len(values)),
            out_specs=jax.tree.map(lambda _: vmem, out_shape),
            scratch_shapes=scratch,
            cost_estimate=pl.CostEstimate(flops=5 * 10**9, bytes_accessed=4 * 2**20, transcendentals=0),
            compiler_params=pltpu.CompilerParams(vmem_limit_bytes=(24 if small else 50) * 2**20),
        )(*carried, *groups_in, *values)

    def orbitals_of(pick, groups_in):
        count = len(groups_in)
        return pl.pallas_call(
            functools.partial(orbitals_kernel, count, shapes, where),
            out_shape=[grid_shape] * count,
            in_specs=[vmem] * (1 + count + len(values)),
            out_specs=[vmem] * count,
            scratch_shapes=[
                pltpu.VMEM((4, n_place, count * lanes), jnp.float32),
                pltpu.VMEM((4, n_picked, count * lanes), jnp.float32),
            ],
            cost_estimate=pl.CostEstimate(flops=10**9, bytes_accessed=2**20, transcendentals=0),
            compiler_params=pltpu.CompilerParams(vmem_limit_bytes=24 * 2**20),
        )(pick, *groups_in, *values)

    if small and batch == members:
        pick, orbs, field = call(
            (2,), indices, (coefs, mate), (pick_shape, grid_shape, grid_shape), begins=True
        )
        near, far = orbitals_of(pick, (got[0], got[1]))
        last = swap(near, "band", lambda at: at ^ 1)
        field = call((2,), (pick, orbs, field), (near, far), grid_shape, ready=True)
        result = call((1,), (pick, orbs, field), (last,), out_shape, ends=True, ready=True)
    else:
        last = swap(got[0], "band", lambda at: at ^ 1)

        def exchange(pieces):
            return call((2, 2, 1), indices, pieces, out_shape, begins=True, ends=True)

        def cut(piece):
            return piece.reshape(owners, -1, batch * points, per_owner).swapaxes(0, 1)

        pieces = (coefs, mate, got[0], got[1], last)
        if batch == members:
            result = exchange(pieces)
        else:
            result = lax.map(exchange, tuple(cut(piece) for piece in pieces))
    return result.reshape(groups, members, points, per_owner)


def solution(mesh):
    return jax.shard_map(
        shards,
        mesh=mesh,
        in_specs=(P("band", None, None, "pw"), P(None, "pw"), P("pw")),
        out_specs=P("band", None, None, "pw"),
        check_vma=False,
    )
```

```python
import functools
import math

import jax
import jax.numpy as jnp
import ml_dtypes
import numpy as np
from jax import lax
from jax.experimental import pallas as pl
from jax.experimental.pallas import tpu as pltpu
from jax.sharding import PartitionSpec as P

HALF = 2
kernel_scale = 4.0
screen_width = 16.0
LANES = 128
ROWS = 16
SMALL = 512
PARITIES = ("cc", "sc", "cs", "ss")


def round_up(value, unit):
    return -(-value // unit) * unit


def split_table(table):
    head = table.astype(np.float32).astype(ml_dtypes.bfloat16)
    rest = (table - head.astype(np.float64)).astype(np.float32).astype(ml_dtypes.bfloat16)
    return head, rest


@functools.lru_cache(maxsize=None)
def build_tables(points, sticks, members):
    signed = np.arange(points)
    signed = np.where(signed < points // 2, signed, signed - points)
    radius = signed[:, None] ** 2 + signed[None, :] ** 2
    limit = np.sort(radius.reshape(-1))[min(sticks, points * points) - 1]
    picked = sorted({(abs(b), abs(c)) for b in signed for c in signed if b * b + c * c <= limit})
    largest = max(b for b, _ in picked)
    grid = 4 * largest + 1 if 4 * largest + 1 < points else points

    def fold(value):
        value = value % points
        return min(value, points - value)

    pairs = set()
    for b1, c1 in picked:
        for b2, c2 in picked:
            for b in {fold(b1 + b2), fold(b1 - b2)}:
                for c in {fold(c1 + c2), fold(c1 - c2)}:
                    pairs.add((b, c))
    near = grid // 2 + 1

    def mirrored(value):
        return 2 * value % grid != 0

    def order(spots):
        return sorted(spots, key=lambda spot: (not mirrored(spot[0]), not mirrored(spot[1]), spot))

    pairs = order(pairs)
    place = order((y, z) for y in range(near) for z in range(near))
    place_weight = np.array([np.prod([1.0 if mirrored(v) else 0.5 for v in spot]) for spot in place])
    small = len(place) <= SMALL

    def wave(kind, freq, spot):
        angle = 2.0 * np.pi * ((freq[:, None] * spot[None, :]) % grid) / grid
        return np.cos(angle) if kind == "c" else np.sin(angle)

    def class_waves(kinds, freqs):
        freqs, spots = np.array(freqs), np.array(place)
        first = wave(kinds[0], freqs[:, 0], spots[:, 0])
        return first * wave(kinds[1], freqs[:, 1], spots[:, 1])

    def class_pairs(kinds):
        if not small:
            return pairs
        if kinds == "cs":
            return [(c, b) for b, c in class_pairs("sc")]
        return [p for p in pairs if all(kind == "c" or mirrored(v) for kind, v in zip(kinds, p))]

    def split_columns(table, rows, cols):
        full = np.zeros((rows, cols))
        full[: table.shape[0], : table.shape[1]] = table
        high, low = split_table(full)
        return np.concatenate([high, low, high], axis=1)

    n_place = round_up(len(place), ROWS)
    n_pairs = round_up(len(pairs), ROWS)
    n_picked = round_up(len(picked), ROWS)
    scale = points**-1.5
    by_parity = dict(synth=[], project=[], forward=[], inverse=[])
    for kinds in PARITIES:
        few = class_waves(kinds, picked)
        many = class_waves(kinds, class_pairs(kinds))
        rows, depth = n_pairs, n_place
        if small:
            rows = round_up(many.shape[0], ROWS)
            depth = round_up(1 + np.flatnonzero(np.abs(many).max(axis=0) > 1e-9)[-1], ROWS)
        few_back = -few * place_weight * scale * (points / grid) ** 2
        by_parity["synth"].append(split_columns(few.T * scale, n_place, n_picked))
        by_parity["project"].append(split_columns(few_back, n_picked, n_place))
        by_parity["forward"].append(split_columns((many * place_weight)[:, :depth], rows, depth))
        by_parity["inverse"].append(split_columns(many.T, n_place, rows))

    index = np.arange(points)
    angle = 2.0 * np.pi * ((index[:, None] * index[None, :]) % points) / points
    cas = np.cos(angle) + np.sin(angle)
    lanes = round_up(members * points, LANES)
    block = np.zeros((lanes, lanes))
    for member in range(members):
        at = member * points
        block[at : at + points, at : at + points] = cas
    high, low = split_table(block)
    turn_left = np.concatenate([high, low, high], axis=1)
    turn_right = np.block([[high, low], [high, low]])

    squares = signed.astype(np.float64) ** 2
    freqs = np.array(pairs)
    total = (freqs[:, 0] ** 2 + freqs[:, 1] ** 2)[:, None] + squares[None, :]
    scaled = total / screen_width
    safe = np.where(total > 0, scaled, 1.0)
    kernel = kernel_scale * np.where(total > 0, -np.expm1(-safe) / safe, 1.0)
    double = np.where(mirrored(freqs), 2.0, 1.0)
    kernel = kernel * (double[:, 0] * double[:, 1])[:, None]
    kernel = kernel * (points / grid) ** 2 / float(points**3)
    weights = np.zeros((n_pairs, lanes))
    for member in range(members):
        weights[: len(pairs), member * points : (member + 1) * points] = kernel

    codes = np.full((n_picked, LANES), -7.0)
    for at, (b, c) in enumerate(picked):
        codes[at, 0], codes[at, 1] = b, c
    tables = dict(
        turn_left=turn_left,
        turn_right=turn_right,
        weights=np.concatenate(split_table(weights), axis=1),
        codes=codes.astype(ml_dtypes.bfloat16),
    )
    for name, each in by_parity.items():
        if small:
            tables.update({name + str(at): table for at, table in enumerate(each)})
        else:
            tables[name] = np.stack(each)
    return tables, small


def pack_tables(tables):
    parities = [str(at) for at in range(len(PARITIES))]
    shelves = [("forward" + at,) for at in parities] + [("project" + at,) for at in parities]
    shelves += [("inverse" + at, "synth" + at) for at in parities]
    shelves.append(("turn_left", "turn_right", "weights", "codes"))
    where, row, width = {}, 0, 0
    for shelf in shelves:
        column = 0
        for name in shelf:
            where[name] = (row, column)
            column += round_up(tables[name].shape[1], LANES)
        row += round_up(max(tables[name].shape[0] for name in shelf), ROWS)
        width = max(width, column)
    packed = np.zeros((row, width), ml_dtypes.bfloat16)
    for name, (first, column) in where.items():
        rows, cols = tables[name].shape
        packed[first : first + rows, column : column + cols] = tables[name]
    return packed, where


def table_getter(shapes, refs, where):
    def get(name, at=None):
        if where is None:
            ref = refs[list(shapes).index(name)]
            return ref[...] if at is None else ref[at]
        name = name if at is None else name + str(at)
        (first, column), (rows, cols) = where[name], shapes[name]
        return refs[0][first : first + rows, column : column + cols]

    return get


def dot(left, right):
    return jnp.dot(left, right, preferred_element_type=jnp.float32)


def split(value):
    high = value.astype(jnp.bfloat16)
    low = (value - high.astype(jnp.float32)).astype(jnp.bfloat16)
    return high, low


def stacked(value):
    high, low = split(value)
    return jnp.concatenate([high, high, low], axis=0)


def product(table, value):
    depth, lanes = value.shape
    if lanes > LANES or depth <= LANES:
        return dot(table, stacked(value))
    halves = jnp.concatenate(split(value), axis=1)
    out = dot(table[:, : 2 * depth], jnp.concatenate([halves, halves], axis=0))
    return out[:, :lanes] + out[:, lanes:]


def pick_matrix(indices, codes, points):
    first, second = indices[0:1], indices[1:2]
    alive = first >= 0.0
    signed_first = jnp.where(first < points // 2, first, first - points)
    signed_second = jnp.where(second < points // 2, second, second - points)
    first_same = codes[:, 0:1] == jnp.where(alive, jnp.abs(signed_first), -1.0)
    one = jnp.where(first_same & (codes[:, 1:2] == jnp.abs(signed_second)), 1.0, 0.0)
    sign_first = jnp.where(signed_first < 0.0, -1.0, 1.0)
    sign_second = jnp.where(signed_second < 0.0, -1.0, 1.0)
    parts = [one, one * sign_first, one * sign_second, one * (sign_first * sign_second)]
    return jnp.concatenate(parts, axis=0).astype(jnp.bfloat16)


def unfold(parts):
    even, odd = parts[0] + parts[2], parts[1] + parts[3]
    even_less, odd_less = parts[0] - parts[2], parts[1] - parts[3]
    return [even + odd, even - odd, even_less + odd_less, even_less - odd_less]


def turn(value, turn_right):
    lanes = turn_right.shape[0] // 2
    outs = []
    for at in range(0, value.shape[1], lanes):
        high, low = split(value[:, at : at + lanes])
        out = dot(jnp.concatenate([high, low], axis=1), turn_right)
        outs.append(out[:, :lanes] + out[:, lanes:])
    return outs[0] if len(outs) == 1 else jnp.concatenate(outs, axis=1)


def each_part(small, body):
    if small:
        for at in range(4):
            body(at)
    else:
        pl.loop(0, 4)(body)


def synthesize(small, blocks, pick, get, coefs_ref, orbs_ref):
    turn_left = get("turn_left")
    fields = [dot(turn_left, stacked(block)) for block in blocks]
    field = fields[0] if len(fields) == 1 else jnp.concatenate(fields, axis=0)
    high, low = split(field)
    contract = (((1,), (1,)), ((), ()))
    coefs = lax.dot_general(pick, high, contract, preferred_element_type=jnp.float32)
    coefs = coefs + lax.dot_general(pick, low, contract, preferred_element_type=jnp.float32)
    rows = pick.shape[0] // 4
    for at in range(4):
        coefs_ref[at] = coefs[at * rows : (at + 1) * rows]

    def body(at):
        orbs_ref[at] = product(get("synth", at), coefs_ref[at])

    each_part(small, body)
    for at, quadrant in enumerate(unfold([orbs_ref[at] for at in range(4)])):
        orbs_ref[at] = quadrant


def read_coefs(ref, lanes):
    block = jnp.concatenate([ref[at] for at in range(ref.shape[0])], axis=1)
    pad = lanes - block.shape[0]
    if pad:
        block = jnp.concatenate([block, jnp.zeros((pad, block.shape[1]), block.dtype)], axis=0)
    return block


def orbitals_kernel(count, shapes, where, pick_ref, *refs):
    get = table_getter(shapes, refs[count:-count - 2], where)
    out_refs, (all_ref, coefs_ref) = refs[-count - 2 : -2], refs[-2:]
    lanes = get("turn_right").shape[0] // 2
    blocks = [read_coefs(ref, lanes) for ref in refs[:count]]
    synthesize(True, blocks, pick_ref[...], get, coefs_ref, all_ref)
    for at in range(4):
        for block, out_ref in enumerate(out_refs):
            out_ref[at] = all_ref[at, :, block * lanes : (block + 1) * lanes]


def exchange_kernel(members, points, owners, sizes, begins, ends, ready, shapes, where, *refs):
    refs = list(refs)
    take = lambda count: [refs.pop(0) for _ in range(count)]
    prior_ref = None
    if begins:
        indices_refs = take(owners)
    else:
        pick_ref, own_ref, prior_ref = take(3)
    coef_refs = take(sum(sizes))
    get = table_getter(shapes, take(len(shapes) if where is None else 1), where)
    if ends:
        (out_ref,) = take(1)
    elif begins:
        pick_ref, own_ref, field_ref = take(3)
    else:
        (field_ref,) = take(1)
    visit_all_ref, work_all_ref, coefs_all_ref = take(3)
    if ends and ready:
        held_ref, semaphores = take(2)
    if begins and ends:
        pick_ref, own_ref, field_ref = take(3)
    if begins:
        pick_ref[...] = pick_matrix(jnp.concatenate([ref[...] for ref in indices_refs], axis=1), get("codes").astype(jnp.float32), points)
    pick, turn_right = pick_ref[...], get("turn_right")
    lanes = turn_right.shape[0] // 2
    small = where is not None
    weight = get("weights").astype(jnp.float32)
    weight = weight[:, :lanes] + weight[:, lanes:]
    start = 0
    for step, size in enumerate(sizes):
        refs = [ref.at[:, :, : size * lanes] for ref in (visit_all_ref, work_all_ref, coefs_all_ref)]
        visit_ref, work_ref, coefs_ref = refs
        group_refs = coef_refs[start : start + size]
        start += size
        if ready:
            visit = [jnp.concatenate([ref[at] for ref in group_refs], axis=1) for at in range(4)]
        else:
            blocks = [read_coefs(ref, lanes) for ref in group_refs]
            synthesize(small, blocks, pick, get, coefs_ref, visit_ref)
            visit = [visit_ref[at] for at in range(4)]
        if begins and step == 0:
            for at in range(4):
                own_ref[at] = visit_ref[at, :, :lanes]
        weights = jnp.concatenate([weight] * size, axis=1)
        density = []
        for at in range(4):
            density.append(jnp.concatenate([own_ref[at]] * size, axis=1) * visit[at])
        density = unfold(density)
        if small:
            stages = (
                lambda at, part: product(get("forward", at), part[: get("forward", at).shape[1] // 3]),
                lambda at, part: turn(part, turn_right) * weights[: part.shape[0]],
                lambda at, part: turn(part, turn_right),
                lambda at, part: product(get("inverse", at), part),
            )
            potential = density
            for stage in stages:
                potential = [stage(at, part) for at, part in enumerate(potential)]
        else:
            for at, part in enumerate(density):
                work_ref[at] = part

            @pl.loop(0, 4)
            def poisson(at):
                spectrum = turn(product(get("forward", at), work_ref[at]), turn_right)
                spectrum = turn(spectrum * weights, turn_right)
                work_ref[at] = product(get("inverse", at), spectrum)

            potential = [work_ref[at] for at in range(4)]
        field = []
        for at, quadrant in enumerate(unfold(potential)):
            term = quadrant * visit[at]
            total = term[:, :lanes]
            for block in range(1, size):
                total = total + term[:, block * lanes : (block + 1) * lanes]
            if prior_ref is not None:
                total = total + prior_ref[at]
            if ends and step == len(sizes) - 1:
                field.append(total)
            else:
                field_ref[at] = total
        if not (ends and step == len(sizes) - 1):
            prior_ref = field_ref
    if ends:
        field = unfold(field)
        coefs = [product(get("project", at), field[at]) for at in range(4)]
        coefs = turn(jnp.concatenate(coefs, axis=0), turn_right)
        high, low = split(coefs.T)
        own_pick = pick[:, : out_ref.shape[1]]
        if not ready:
            out_ref[...] = (dot(high, own_pick) + dot(low, own_pick))[: members * points]
            return
        copies = []
        for member in range(members):
            here = slice(member * points, (member + 1) * points)
            held_ref[here] = dot(high[here], own_pick) + dot(low[here], own_pick)
            copies.append(
                pltpu.make_async_copy(held_ref.at[here], out_ref.at[here], semaphores.at[member])
            )
            copies[-1].start()
        for copy in copies:
            copy.wait()


def hold_kernel(*refs):
    semaphores = refs[-1]
    count = (len(refs) - 1) // 2
    copies = [
        pltpu.make_async_copy(refs[at], refs[count + at], semaphores.at[at]) for at in range(count)
    ]
    for copy in copies:
        copy.start()
    for copy in copies:
        copy.wait()


def hold(*values, flops=0):
    return pl.pallas_call(
        hold_kernel,
        out_shape=[jax.ShapeDtypeStruct(value.shape, value.dtype) for value in values],
        in_specs=[pl.BlockSpec(memory_space=pl.ANY)] * len(values),
        out_specs=[pl.BlockSpec(memory_space=pltpu.VMEM)] * len(values),
        scratch_shapes=[pltpu.SemaphoreType.DMA((len(values),))],
        cost_estimate=pl.CostEstimate(flops=flops, bytes_accessed=2**16, transcendentals=0),
        compiler_params=pltpu.CompilerParams(vmem_limit_bytes=16 * 2**20),
    )(*values)


def swap(value, axis, partner):
    count = lax.axis_size(axis)
    return lax.ppermute(value, axis, [(at, partner(at) % count) for at in range(count)])


def rest_of_ring(value, axis):
    count = lax.axis_size(axis)
    return [
        lax.ppermute(value, axis, [(at, (at + step) % count) for at in range(count)])
        for step in range(1, count)
    ]


def shards(stick_coefs, miller, stick_count):
    groups, members, points, per_owner = stick_coefs.shape
    owners = lax.axis_size("pw")
    batch = max(n for n in range(1, members + 1) if members % n == 0 and (n == 1 or n * points <= LANES))
    tables, small = build_tables(points, per_owner * owners, batch)
    shapes = {name: table.shape for name, table in tables.items()}
    where, held = None, list(tables.values())
    if small:
        packed, where = pack_tables(tables)
        held = [packed]
    values = [jnp.asarray(table) for table in held]
    own = stick_coefs.reshape(members * points, per_owner)
    others = rest_of_ring(own, "pw")
    early = swap(own, "band", lambda at: at ^ 1)
    position = jnp.arange(per_owner, dtype=jnp.int32)[None]
    indices = jnp.where(position < stick_count[0], miller, -1).astype(jnp.float32)
    indices = jnp.concatenate([indices, jnp.zeros((6, per_owner), jnp.float32)], axis=0)
    other_indices = rest_of_ring(indices, "pw")
    (own,) = hold(own)
    (indices,) = hold(indices, flops=5 * 10**9)
    indices = [indices] + other_indices

    ring = lax.axis_size("band")
    coefs = jnp.stack([own] + others)
    mate = jnp.stack([early] + [swap(other, "band", lambda at: at ^ 1) for other in others])
    got = swap(jnp.stack([coefs, mate]), "band", lambda at: at + 1 if at & 1 else at - 1 + ring)

    lanes = tables["turn_right"].shape[0] // 2
    n_place, n_picked = shapes["synth0" if small else "synth"][-2], shapes["codes"][0]
    vmem = pl.BlockSpec(memory_space=pltpu.VMEM)
    grid_shape = jax.ShapeDtypeStruct((4, n_place, lanes), jnp.float32)

    pick_shape = jax.ShapeDtypeStruct((4 * n_picked, per_owner * owners), jnp.bfloat16)
    out_shape = jax.ShapeDtypeStruct((batch * points, per_owner), jnp.float32)

    def call(sizes, carried, groups_in, out_shape, begins=False, ends=False, ready=False):
        wide = max(sizes) * lanes
        scratch = [
            pltpu.VMEM((4, n_place, wide), jnp.float32),
            pltpu.VMEM((4, 8 if small else n_place, wide), jnp.float32),
            pltpu.VMEM((4, n_picked, wide), jnp.float32),
        ]
        if begins and ends:
            scratch += [pltpu.VMEM(each.shape, each.dtype) for each in (pick_shape, grid_shape, grid_shape)]
        if ends and ready:
            scratch += [
                pltpu.VMEM(out_shape.shape, out_shape.dtype),
                pltpu.SemaphoreType.DMA((batch,)),
            ]
        return pl.pallas_call(
            functools.partial(
                exchange_kernel, batch, points, owners, sizes, begins, ends, ready, shapes, where
            ),
            out_shape=out_shape,
            in_specs=[vmem] * (len(carried) + len(groups_in) + len(values)),
            out_specs=jax.tree.map(
                lambda _: pl.BlockSpec(memory_space=pl.ANY) if ends and ready else vmem, out_shape
            ),
            scratch_shapes=scratch,
            cost_estimate=pl.CostEstimate(flops=5 * 10**9, bytes_accessed=4 * 2**20, transcendentals=0),
            compiler_params=pltpu.CompilerParams(vmem_limit_bytes=(24 if small else 50) * 2**20),
        )(*carried, *groups_in, *values)

    def orbitals_of(pick, groups_in):
        count = len(groups_in)
        return pl.pallas_call(
            functools.partial(orbitals_kernel, count, shapes, where),
            out_shape=[grid_shape] * count,
            in_specs=[vmem] * (1 + count + len(values)),
            out_specs=[vmem] * count,
            scratch_shapes=[
                pltpu.VMEM((4, n_place, count * lanes), jnp.float32),
                pltpu.VMEM((4, n_picked, count * lanes), jnp.float32),
            ],
            cost_estimate=pl.CostEstimate(flops=10**9, bytes_accessed=2**20, transcendentals=0),
            compiler_params=pltpu.CompilerParams(vmem_limit_bytes=24 * 2**20),
        )(pick, *groups_in, *values)

    if small and batch == members:
        pick, orbs, field = call(
            (2,), indices, (coefs, mate), (pick_shape, grid_shape, grid_shape), begins=True
        )
        near, far = orbitals_of(pick, (got[0], got[1]))
        last = swap(near, "band", lambda at: at ^ 1)
        field = call((2,), (pick, orbs, field), (near, far), grid_shape, ready=True)
        result = call((1,), (pick, orbs, field), (last,), out_shape, ends=True, ready=True)
    else:
        last = swap(got[0], "band", lambda at: at ^ 1)

        def exchange(pieces):
            return call((2, 2, 1), indices, pieces, out_shape, begins=True, ends=True)

        def cut(piece):
            return piece.reshape(owners, -1, batch * points, per_owner).swapaxes(0, 1)

        pieces = (coefs, mate, got[0], got[1], last)
        if batch == members:
            result = exchange(pieces)
        else:
            result = lax.map(exchange, tuple(cut(piece) for piece in pieces))
    return result.reshape(groups, members, points, per_owner)


def solution(mesh):
    return jax.shard_map(
        shards,
        mesh=mesh,
        in_specs=(P("band", None, None, "pw"), P(None, "pw"), P("pw")),
        out_specs=P("band", None, None, "pw"),
        check_vma=False,
    )
```

```python
import functools
import math

import jax
import jax.numpy as jnp
import ml_dtypes
import numpy as np
from jax import lax
from jax.experimental import pallas as pl
from jax.experimental.pallas import tpu as pltpu
from jax.sharding import PartitionSpec as P

HALF = 2
kernel_scale = 4.0
screen_width = 16.0
LANES = 128
ROWS = 16
SMALL = 512
PARITIES = ("cc", "sc", "cs", "ss")


def round_up(value, unit):
    return -(-value // unit) * unit


def split_table(table):
    head = table.astype(np.float32).astype(ml_dtypes.bfloat16)
    rest = (table - head.astype(np.float64)).astype(np.float32).astype(ml_dtypes.bfloat16)
    return head, rest


@functools.lru_cache(maxsize=None)
def build_tables(points, sticks, members):
    signed = np.arange(points)
    signed = np.where(signed < points // 2, signed, signed - points)
    radius = signed[:, None] ** 2 + signed[None, :] ** 2
    limit = np.sort(radius.reshape(-1))[min(sticks, points * points) - 1]
    picked = sorted({(abs(b), abs(c)) for b in signed for c in signed if b * b + c * c <= limit})
    largest = max(b for b, _ in picked)
    grid = 4 * largest + 1 if 4 * largest + 1 < points else points

    def fold(value):
        value = value % points
        return min(value, points - value)

    pairs = set()
    for b1, c1 in picked:
        for b2, c2 in picked:
            for b in {fold(b1 + b2), fold(b1 - b2)}:
                for c in {fold(c1 + c2), fold(c1 - c2)}:
                    pairs.add((b, c))
    near = grid // 2 + 1

    def mirrored(value):
        return 2 * value % grid != 0

    def order(spots):
        return sorted(spots, key=lambda spot: (not mirrored(spot[0]), not mirrored(spot[1]), spot))

    pairs = order(pairs)
    place = order((y, z) for y in range(near) for z in range(near))
    place_weight = np.array([np.prod([1.0 if mirrored(v) else 0.5 for v in spot]) for spot in place])
    small = len(place) <= SMALL

    def wave(kind, freq, spot):
        angle = 2.0 * np.pi * ((freq[:, None] * spot[None, :]) % grid) / grid
        return np.cos(angle) if kind == "c" else np.sin(angle)

    def class_waves(kinds, freqs):
        freqs, spots = np.array(freqs), np.array(place)
        first = wave(kinds[0], freqs[:, 0], spots[:, 0])
        return first * wave(kinds[1], freqs[:, 1], spots[:, 1])

    def class_pairs(kinds):
        if not small:
            return pairs
        if kinds == "cs":
            return [(c, b) for b, c in class_pairs("sc")]
        return [p for p in pairs if all(kind == "c" or mirrored(v) for kind, v in zip(kinds, p))]

    def split_columns(table, rows, cols):
        full = np.zeros((rows, cols))
        full[: table.shape[0], : table.shape[1]] = table
        high, low = split_table(full)
        return np.concatenate([high, low, high], axis=1)

    n_place = round_up(len(place), ROWS)
    n_pairs = round_up(len(pairs), ROWS)
    n_picked = round_up(len(picked), ROWS)
    scale = points**-1.5
    by_parity = dict(synth=[], project=[], forward=[], inverse=[])
    for kinds in PARITIES:
        few = class_waves(kinds, picked)
        many = class_waves(kinds, class_pairs(kinds))
        rows, depth = n_pairs, n_place
        if small:
            rows = round_up(many.shape[0], ROWS)
            depth = round_up(1 + np.flatnonzero(np.abs(many).max(axis=0) > 1e-9)[-1], ROWS)
        few_back = -few * place_weight * scale * (points / grid) ** 2
        by_parity["synth"].append(split_columns((few.T * scale)[:depth], depth, n_picked))
        by_parity["project"].append(split_columns(few_back, n_picked, n_place))
        by_parity["forward"].append(split_columns((many * place_weight)[:, :depth], rows, depth))
        by_parity["inverse"].append(split_columns(many.T[:depth], depth, rows))

    index = np.arange(points)
    angle = 2.0 * np.pi * ((index[:, None] * index[None, :]) % points) / points
    cas = np.cos(angle) + np.sin(angle)
    lanes = round_up(members * points, LANES)
    block = np.zeros((lanes, lanes))
    for member in range(members):
        at = member * points
        block[at : at + points, at : at + points] = cas
    high, low = split_table(block)
    turn_left = np.concatenate([high, low, high], axis=1)
    turn_right = np.block([[high, low], [high, low]])

    squares = signed.astype(np.float64) ** 2
    freqs = np.array(pairs)
    total = (freqs[:, 0] ** 2 + freqs[:, 1] ** 2)[:, None] + squares[None, :]
    scaled = total / screen_width
    safe = np.where(total > 0, scaled, 1.0)
    kernel = kernel_scale * np.where(total > 0, -np.expm1(-safe) / safe, 1.0)
    double = np.where(mirrored(freqs), 2.0, 1.0)
    kernel = kernel * (double[:, 0] * double[:, 1])[:, None]
    kernel = kernel * (points / grid) ** 2 / float(points**3)
    weights = np.zeros((n_pairs, lanes))
    for member in range(members):
        weights[: len(pairs), member * points : (member + 1) * points] = kernel

    codes = np.full((n_picked, LANES), -7.0)
    for at, (b, c) in enumerate(picked):
        codes[at, 0], codes[at, 1] = b, c
    tables = dict(
        turn_left=turn_left,
        turn_right=turn_right,
        weights=np.concatenate(split_table(weights), axis=1),
        codes=codes.astype(ml_dtypes.bfloat16),
    )
    for name, each in by_parity.items():
        if small:
            tables.update({name + str(at): table for at, table in enumerate(each)})
        else:
            tables[name] = np.stack(each)
    return tables, small


def pack_tables(tables):
    parities = [str(at) for at in range(len(PARITIES))]
    shelves = [("forward" + at,) for at in parities] + [("project" + at,) for at in parities]
    shelves += [("inverse" + at, "synth" + at) for at in parities]
    shelves.append(("turn_left", "turn_right", "weights", "codes"))
    where, row, width = {}, 0, 0
    for shelf in shelves:
        column = 0
        for name in shelf:
            where[name] = (row, column)
            column += round_up(tables[name].shape[1], LANES)
        row += round_up(max(tables[name].shape[0] for name in shelf), ROWS)
        width = max(width, column)
    packed = np.zeros((row, width), ml_dtypes.bfloat16)
    for name, (first, column) in where.items():
        rows, cols = tables[name].shape
        packed[first : first + rows, column : column + cols] = tables[name]
    return packed, where


def table_getter(shapes, refs, where):
    def get(name, at=None):
        if where is None:
            ref = refs[list(shapes).index(name)]
            return ref[...] if at is None else ref[at]
        name = name if at is None else name + str(at)
        (first, column), (rows, cols) = where[name], shapes[name]
        return refs[0][first : first + rows, column : column + cols]

    return get


def dot(left, right):
    return jnp.dot(left, right, preferred_element_type=jnp.float32)


def split(value):
    high = value.astype(jnp.bfloat16)
    low = (value - high.astype(jnp.float32)).astype(jnp.bfloat16)
    return high, low


def stacked(value):
    high, low = split(value)
    return jnp.concatenate([high, high, low], axis=0)


def product(table, value):
    depth, lanes = value.shape
    if lanes > LANES or depth <= LANES:
        return dot(table, stacked(value))
    halves = jnp.concatenate(split(value), axis=1)
    out = dot(table[:, : 2 * depth], jnp.concatenate([halves, halves], axis=0))
    return out[:, :lanes] + out[:, lanes:]


def fill_rows(value, rows):
    missing = rows - value.shape[0]
    if not missing:
        return value
    return jnp.concatenate([value, jnp.zeros((missing, value.shape[1]), value.dtype)], axis=0)


def pick_matrix(indices, codes, points):
    first, second = indices[0:1], indices[1:2]
    alive = first >= 0.0
    signed_first = jnp.where(first < points // 2, first, first - points)
    signed_second = jnp.where(second < points // 2, second, second - points)
    first_same = codes[:, 0:1] == jnp.where(alive, jnp.abs(signed_first), -1.0)
    one = jnp.where(first_same & (codes[:, 1:2] == jnp.abs(signed_second)), 1.0, 0.0)
    sign_first = jnp.where(signed_first < 0.0, -1.0, 1.0)
    sign_second = jnp.where(signed_second < 0.0, -1.0, 1.0)
    parts = [one, one * sign_first, one * sign_second, one * (sign_first * sign_second)]
    return jnp.concatenate(parts, axis=0).astype(jnp.bfloat16)


def unfold(parts):
    even, odd = parts[0] + parts[2], parts[1] + parts[3]
    even_less, odd_less = parts[0] - parts[2], parts[1] - parts[3]
    return [even + odd, even - odd, even_less + odd_less, even_less - odd_less]


def turn(value, turn_right):
    lanes = turn_right.shape[0] // 2
    outs = []
    for at in range(0, value.shape[1], lanes):
        high, low = split(value[:, at : at + lanes])
        out = dot(jnp.concatenate([high, low], axis=1), turn_right)
        outs.append(out[:, :lanes] + out[:, lanes:])
    return outs[0] if len(outs) == 1 else jnp.concatenate(outs, axis=1)


def each_part(small, body):
    if small:
        for at in range(4):
            body(at)
    else:
        pl.loop(0, 4)(body)


def synthesize(small, blocks, pick, get, coefs_ref, orbs_ref):
    turn_left = get("turn_left")
    fields = [dot(turn_left, stacked(block)) for block in blocks]
    field = fields[0] if len(fields) == 1 else jnp.concatenate(fields, axis=0)
    high, low = split(field)
    contract = (((1,), (1,)), ((), ()))
    coefs = lax.dot_general(pick, high, contract, preferred_element_type=jnp.float32)
    coefs = coefs + lax.dot_general(pick, low, contract, preferred_element_type=jnp.float32)
    rows = pick.shape[0] // 4
    for at in range(4):
        coefs_ref[at] = coefs[at * rows : (at + 1) * rows]

    def body(at):
        orbs_ref[at] = fill_rows(product(get("synth", at), coefs_ref[at]), orbs_ref.shape[1])

    each_part(small, body)
    for at, quadrant in enumerate(unfold([orbs_ref[at] for at in range(4)])):
        orbs_ref[at] = quadrant


def read_coefs(ref, lanes):
    block = jnp.concatenate([ref[at] for at in range(ref.shape[0])], axis=1)
    pad = lanes - block.shape[0]
    if pad:
        block = jnp.concatenate([block, jnp.zeros((pad, block.shape[1]), block.dtype)], axis=0)
    return block


def orbitals_kernel(count, shapes, where, pick_ref, *refs):
    get = table_getter(shapes, refs[count:-count - 2], where)
    out_refs, (all_ref, coefs_ref) = refs[-count - 2 : -2], refs[-2:]
    lanes = get("turn_right").shape[0] // 2
    blocks = [read_coefs(ref, lanes) for ref in refs[:count]]
    synthesize(True, blocks, pick_ref[...], get, coefs_ref, all_ref)
    for at in range(4):
        for block, out_ref in enumerate(out_refs):
            out_ref[at] = all_ref[at, :, block * lanes : (block + 1) * lanes]


def exchange_kernel(members, points, owners, sizes, begins, ends, ready, shapes, where, *refs):
    refs = list(refs)
    take = lambda count: [refs.pop(0) for _ in range(count)]
    prior_ref = None
    if begins:
        indices_refs = take(owners)
    else:
        pick_ref, own_ref, prior_ref = take(3)
    coef_refs = take(sum(sizes))
    get = table_getter(shapes, take(len(shapes) if where is None else 1), where)
    if ends:
        (out_ref,) = take(1)
    elif begins:
        pick_ref, own_ref, field_ref = take(3)
    else:
        (field_ref,) = take(1)
    visit_all_ref, work_all_ref, coefs_all_ref = take(3)
    if ends and ready:
        held_ref, semaphores = take(2)
    if begins and ends:
        pick_ref, own_ref, field_ref = take(3)
    if begins:
        pick_ref[...] = pick_matrix(jnp.concatenate([ref[...] for ref in indices_refs], axis=1), get("codes").astype(jnp.float32), points)
    pick, turn_right = pick_ref[...], get("turn_right")
    lanes = turn_right.shape[0] // 2
    small = where is not None
    weight = get("weights").astype(jnp.float32)
    weight = weight[:, :lanes] + weight[:, lanes:]
    start = 0
    for step, size in enumerate(sizes):
        refs = [ref.at[:, :, : size * lanes] for ref in (visit_all_ref, work_all_ref, coefs_all_ref)]
        visit_ref, work_ref, coefs_ref = refs
        group_refs = coef_refs[start : start + size]
        start += size
        if ready:
            visit = [jnp.concatenate([ref[at] for ref in group_refs], axis=1) for at in range(4)]
        else:
            blocks = [read_coefs(ref, lanes) for ref in group_refs]
            synthesize(small, blocks, pick, get, coefs_ref, visit_ref)
            visit = [visit_ref[at] for at in range(4)]
        if begins and step == 0:
            for at in range(4):
                own_ref[at] = visit_ref[at, :, :lanes]
        weights = jnp.concatenate([weight] * size, axis=1)
        density = []
        for at in range(4):
            density.append(jnp.concatenate([own_ref[at]] * size, axis=1) * visit[at])
        density = unfold(density)
        if small:
            stages = (
                lambda at, part: product(get("forward", at), part[: get("forward", at).shape[1] // 3]),
                lambda at, part: turn(part, turn_right) * weights[: part.shape[0]],
                lambda at, part: turn(part, turn_right),
                lambda at, part: fill_rows(product(get("inverse", at), part), visit[at].shape[0]),
            )
            potential = density
            for stage in stages:
                potential = [stage(at, part) for at, part in enumerate(potential)]
        else:
            for at, part in enumerate(density):
                work_ref[at] = part

            @pl.loop(0, 4)
            def poisson(at):
                spectrum = turn(product(get("forward", at), work_ref[at]), turn_right)
                spectrum = turn(spectrum * weights, turn_right)
                work_ref[at] = product(get("inverse", at), spectrum)

            potential = [work_ref[at] for at in range(4)]
        field = []
        for at, quadrant in enumerate(unfold(potential)):
            term = quadrant * visit[at]
            total = term[:, :lanes]
            for block in range(1, size):
                total = total + term[:, block * lanes : (block + 1) * lanes]
            if prior_ref is not None:
                total = total + prior_ref[at]
            if ends and step == len(sizes) - 1:
                field.append(total)
            else:
                field_ref[at] = total
        if not (ends and step == len(sizes) - 1):
            prior_ref = field_ref
    if ends:
        field = unfold(field)
        coefs = [product(get("project", at), field[at]) for at in range(4)]
        coefs = turn(jnp.concatenate(coefs, axis=0), turn_right)
        high, low = split(coefs.T)
        own_pick = pick[:, : out_ref.shape[1]]
        if not ready:
            out_ref[...] = (dot(high, own_pick) + dot(low, own_pick))[: members * points]
            return
        copies = []
        for member in range(members):
            here = slice(member * points, (member + 1) * points)
            held_ref[here] = dot(high[here], own_pick) + dot(low[here], own_pick)
            copies.append(
                pltpu.make_async_copy(held_ref.at[here], out_ref.at[here], semaphores.at[member])
            )
            copies[-1].start()
        for copy in copies:
            copy.wait()


def hold_kernel(*refs):
    semaphores = refs[-1]
    count = (len(refs) - 1) // 2
    copies = [
        pltpu.make_async_copy(refs[at], refs[count + at], semaphores.at[at]) for at in range(count)
    ]
    for copy in copies:
        copy.start()
    for copy in copies:
        copy.wait()


def hold(*values, flops=0):
    return pl.pallas_call(
        hold_kernel,
        out_shape=[jax.ShapeDtypeStruct(value.shape, value.dtype) for value in values],
        in_specs=[pl.BlockSpec(memory_space=pl.ANY)] * len(values),
        out_specs=[pl.BlockSpec(memory_space=pltpu.VMEM)] * len(values),
        scratch_shapes=[pltpu.SemaphoreType.DMA((len(values),))],
        cost_estimate=pl.CostEstimate(flops=flops, bytes_accessed=2**16, transcendentals=0),
        compiler_params=pltpu.CompilerParams(vmem_limit_bytes=16 * 2**20),
    )(*values)


def swap(value, axis, partner):
    count = lax.axis_size(axis)
    return lax.ppermute(value, axis, [(at, partner(at) % count) for at in range(count)])


def rest_of_ring(value, axis):
    count = lax.axis_size(axis)
    return [
        lax.ppermute(value, axis, [(at, (at + step) % count) for at in range(count)])
        for step in range(1, count)
    ]


def shards(stick_coefs, miller, stick_count):
    groups, members, points, per_owner = stick_coefs.shape
    owners = lax.axis_size("pw")
    batch = max(n for n in range(1, members + 1) if members % n == 0 and (n == 1 or n * points <= LANES))
    tables, small = build_tables(points, per_owner * owners, batch)
    shapes = {name: table.shape for name, table in tables.items()}
    where, held = None, list(tables.values())
    if small:
        packed, where = pack_tables(tables)
        held = [packed]
    values = [jnp.asarray(table) for table in held]
    own = stick_coefs.reshape(members * points, per_owner)
    others = rest_of_ring(own, "pw")
    early = swap(own, "band", lambda at: at ^ 1)
    position = jnp.arange(per_owner, dtype=jnp.int32)[None]
    indices = jnp.where(position < stick_count[0], miller, -1).astype(jnp.float32)
    indices = jnp.concatenate([indices, jnp.zeros((6, per_owner), jnp.float32)], axis=0)
    other_indices = rest_of_ring(indices, "pw")
    (own,) = hold(own)
    (indices,) = hold(indices, flops=5 * 10**9)
    indices = [indices] + other_indices

    ring = lax.axis_size("band")
    coefs = jnp.stack([own] + others)
    mate = jnp.stack([early] + [swap(other, "band", lambda at: at ^ 1) for other in others])
    got = swap(jnp.stack([coefs, mate]), "band", lambda at: at + 1 if at & 1 else at - 1 + ring)

    lanes = tables["turn_right"].shape[0] // 2
    n_place, n_picked = shapes["synth0" if small else "synth"][-2], shapes["codes"][0]
    vmem = pl.BlockSpec(memory_space=pltpu.VMEM)
    grid_shape = jax.ShapeDtypeStruct((4, n_place, lanes), jnp.float32)

    pick_shape = jax.ShapeDtypeStruct((4 * n_picked, per_owner * owners), jnp.bfloat16)
    out_shape = jax.ShapeDtypeStruct((batch * points, per_owner), jnp.float32)

    def call(sizes, carried, groups_in, out_shape, begins=False, ends=False, ready=False):
        wide = max(sizes) * lanes
        scratch = [
            pltpu.VMEM((4, n_place, wide), jnp.float32),
            pltpu.VMEM((4, 8 if small else n_place, wide), jnp.float32),
            pltpu.VMEM((4, n_picked, wide), jnp.float32),
        ]
        if begins and ends:
            scratch += [pltpu.VMEM(each.shape, each.dtype) for each in (pick_shape, grid_shape, grid_shape)]
        if ends and ready:
            scratch += [
                pltpu.VMEM(out_shape.shape, out_shape.dtype),
                pltpu.SemaphoreType.DMA((batch,)),
            ]
        return pl.pallas_call(
            functools.partial(
                exchange_kernel, batch, points, owners, sizes, begins, ends, ready, shapes, where
            ),
            out_shape=out_shape,
            in_specs=[vmem] * (len(carried) + len(groups_in) + len(values)),
            out_specs=jax.tree.map(
                lambda _: pl.BlockSpec(memory_space=pl.ANY) if ends and ready else vmem, out_shape
            ),
            scratch_shapes=scratch,
            cost_estimate=pl.CostEstimate(flops=5 * 10**9, bytes_accessed=4 * 2**20, transcendentals=0),
            compiler_params=pltpu.CompilerParams(vmem_limit_bytes=(24 if small else 50) * 2**20),
        )(*carried, *groups_in, *values)

    def orbitals_of(pick, groups_in):
        count = len(groups_in)
        return pl.pallas_call(
            functools.partial(orbitals_kernel, count, shapes, where),
            out_shape=[grid_shape] * count,
            in_specs=[vmem] * (1 + count + len(values)),
            out_specs=[vmem] * count,
            scratch_shapes=[
                pltpu.VMEM((4, n_place, count * lanes), jnp.float32),
                pltpu.VMEM((4, n_picked, count * lanes), jnp.float32),
            ],
            cost_estimate=pl.CostEstimate(flops=10**9, bytes_accessed=2**20, transcendentals=0),
            compiler_params=pltpu.CompilerParams(vmem_limit_bytes=24 * 2**20),
        )(pick, *groups_in, *values)

    if small and batch == members:
        pick, orbs, field = call(
            (2,), indices, (coefs, mate), (pick_shape, grid_shape, grid_shape), begins=True
        )
        near, far = orbitals_of(pick, (got[0], got[1]))
        last = swap(near, "band", lambda at: at ^ 1)
        field = call((2,), (pick, orbs, field), (near, far), grid_shape, ready=True)
        result = call((1,), (pick, orbs, field), (last,), out_shape, ends=True, ready=True)
    else:
        last = swap(got[0], "band", lambda at: at ^ 1)

        def exchange(pieces):
            return call((2, 2, 1), indices, pieces, out_shape, begins=True, ends=True)

        def cut(piece):
            return piece.reshape(owners, -1, batch * points, per_owner).swapaxes(0, 1)

        pieces = (coefs, mate, got[0], got[1], last)
        if batch == members:
            result = exchange(pieces)
        else:
            result = lax.map(exchange, tuple(cut(piece) for piece in pieces))
    return result.reshape(groups, members, points, per_owner)


def solution(mesh):
    return jax.shard_map(
        shards,
        mesh=mesh,
        in_specs=(P("band", None, None, "pw"), P(None, "pw"), P("pw")),
        out_specs=P("band", None, None, "pw"),
        check_vma=False,
    )
```
